32 devices in a mesh: gy: 8 (over y, x, core), gz: 4 (over z).
Axes of the slice: x: 2, y: 2, z: 4, core: 2. Of those that a mesh axis runs over, the one named last changes fastest.
Arguments:
- dual_flow_speeds: float32 [3, 64, 64, 1024], P(None, 'gy', 'gz'), may hold values from -6 to 6
- dual_thermal_state: float32 [64, 64, 1024], P('gy', 'gz'), may hold values from -6 to 6
- forward_flow_speeds: bfloat16 [3, 64, 64, 1024], P(None, 'gy', 'gz'), may hold values from -4 to 4
- forward_thermal_state: bfloat16 [64, 64, 1024], P('gy', 'gz'), may hold values from -6 to 6
Outputs:
- advanced_dual_motion: float32 [3, 64, 64, 1024], P(None, 'gy', 'gz')
- advanced_dual_thermal: float32 [64, 64, 1024], P('gy', 'gz')
The draws below stay inside these ranges and needn't reach their ends.
All inputs are finite; a program needn't handle non-finite values.
Results may differ from the reference program's by a relative error of at most 0.0003.
Values sent between devices are 32-bit elements; how exact they have to be, the bound alone decides.
A program may use at most 128 MiB of HBM per device.

```python
import math
import jax
import jax.numpy as jnp
from jax import lax

LENGTHWISE_SIZE = 1024
SPANWISE_SIZE = 64
VERTICAL_SIZE = 64


def shard_levels(rng, shape, split, low, top_value):
    loudness = 1.0
    for dim, shards_of in split:
        draws = jax.random.uniform(jax.random.fold_in(jax.random.fold_in(rng, 6), dim), (shards_of,), jnp.float32, low / len(split), top_value / len(split))
        loudness = loudness * jnp.repeat(jnp.exp(draws), shape[dim] // shards_of).reshape((-1,) + (1,) * (len(shape) - 1 - dim))
    return loudness


def scatter_about(key, extent, deviation, most, split=(), kind=jnp.bfloat16):
    loudness = shard_levels(key, extent, split, -0.22, 0.18) if split else 1.0
    drawn = jax.random.normal(key, extent, jnp.float32) * deviation * loudness
    return jnp.minimum(jnp.maximum(drawn, -most), most).astype(kind)


def setup_inputs(seed: int = 0) -> dict:
    splits = jax.random.split(jax.random.key(seed), 5)
    return {
        "dual_flow_speeds": scatter_about(splits[0], (3, SPANWISE_SIZE, VERTICAL_SIZE, LENGTHWISE_SIZE), 1.0, 6.0, ((1, 8), (2, 4)), jnp.float32),
        "dual_thermal_state": scatter_about(splits[1], (SPANWISE_SIZE, VERTICAL_SIZE, LENGTHWISE_SIZE), 1.0, 6.0, ((0, 8), (1, 4)), jnp.float32),
        "forward_flow_speeds": scatter_about(splits[2], (3, SPANWISE_SIZE, VERTICAL_SIZE, LENGTHWISE_SIZE), 1.0, 4.0, ((1, 8), (2, 4))),
        "forward_thermal_state": scatter_about(splits[3], (SPANWISE_SIZE, VERTICAL_SIZE, LENGTHWISE_SIZE), 1.0, 6.0, ((0, 8), (1, 4))),
    }


time_step = 0.2
viscosity = 0.1
diffusivity = 0.1
buoyancy = 1.0


def tendency_contributions(haloed_quantities, motion_pieces):
    centre = haloed_quantities[:, 1:-1, 1:-1]
    slope_x = 0.5 * (jnp.roll(centre, -1, axis=3) - jnp.roll(centre, 1, axis=3))
    slope_y = 0.5 * (haloed_quantities[:, 2:, 1:-1] - haloed_quantities[:, :-2, 1:-1])
    slope_z = 0.5 * (haloed_quantities[:, 1:-1, 2:] - haloed_quantities[:, 1:-1, :-2])
    laplace = (jnp.roll(centre[:4], -1, axis=3) + jnp.roll(centre[:4], 1, axis=3)) + (haloed_quantities[:4, 2:, 1:-1] + haloed_quantities[:4, :-2, 1:-1]) + (haloed_quantities[:4, 1:-1, 2:] + haloed_quantities[:4, 1:-1, :-2]) - 6.0 * centre[:4]
    advect = motion_pieces[0] * slope_x[:4] + motion_pieces[1] * slope_y[:4] + motion_pieces[2] * slope_z[:4]
    heat_slope = jnp.stack([slope_x[4], slope_y[4], slope_z[4]])
    unprojected_motion = centre[:3] + time_step * (advect[:3] + viscosity * laplace[:3] + centre[3] * heat_slope)
    thermal_following = centre[3] + time_step * (advect[3] + diffusivity * laplace[3] + buoyancy * centre[2])
    return unprojected_motion, thermal_following


def hartley(field, axis):
    transformed = jnp.fft.fft(field, axis=axis)
    return transformed.real - transformed.imag


def cosine_table(length):
    indices = jnp.arange(length, dtype=jnp.int32)
    phases = (indices[None, :] * (2 * indices[:, None] + 1)) % (4 * length)
    return jnp.cos(phases.astype(jnp.float32) * (math.pi / (2 * length)))


def cosine_inverse(length):
    indices = jnp.arange(length, dtype=jnp.int32)
    weights = jnp.where(indices == 0, 1.0, 2.0).astype(jnp.float32)
    return cosine_table(length).T * weights[:, None] / length


def eigen_periodic(waves, length):
    return 2.0 - 2.0 * jnp.cos(waves.astype(jnp.float32) * (2.0 * math.pi / length))


def eigen_wall(waves, length):
    return 2.0 - 2.0 * jnp.cos(waves.astype(jnp.float32) * (math.pi / length))


def reference(dual_flow_speeds, dual_thermal_state, forward_flow_speeds, forward_thermal_state):
    quantity_bundle = jnp.concatenate([dual_flow_speeds, dual_thermal_state[None], forward_thermal_state[None].astype(jnp.float32)], 0)
    haloed_quantities = jnp.concatenate([quantity_bundle[:, -1:], quantity_bundle, quantity_bundle[:, :1]], axis=1)
    haloed_quantities = jnp.pad(haloed_quantities, ((0, 0), (0, 0), (1, 1), (0, 0)))
    motion_pieces = forward_flow_speeds.astype(jnp.float32)
    block_rows = math.gcd(SPANWISE_SIZE, 64)
    parts_pre = []
    thermal_pieces = []
    for start in range(0, SPANWISE_SIZE, block_rows):
        unprojected_motion, thermal_following = tendency_contributions(haloed_quantities[:, start:start + block_rows + 2], motion_pieces[:, start:start + block_rows])
        parts_pre.append(unprojected_motion)
        thermal_pieces.append(thermal_following)
    unprojected_motion = jnp.concatenate(parts_pre, 1)
    advanced_dual_thermal = jnp.concatenate(thermal_pieces, 0)
    next_z = jnp.concatenate([unprojected_motion[2][:, 1:], jnp.zeros((SPANWISE_SIZE, 1, LENGTHWISE_SIZE), jnp.float32)], 1)
    source = (jnp.roll(unprojected_motion[0], -1, axis=2) - unprojected_motion[0]) + (jnp.roll(unprojected_motion[1], -1, axis=0) - unprojected_motion[1]) + (next_z - unprojected_motion[2])
    spectral = hartley(hartley(source, 2), 0)
    spectral = jnp.einsum('yzx,zk->ykx', spectral, cosine_table(VERTICAL_SIZE), precision=lax.Precision.HIGHEST)
    eigen_sum = eigen_periodic(jnp.arange(LENGTHWISE_SIZE, dtype=jnp.int32), LENGTHWISE_SIZE)[None, None, :] + eigen_periodic(jnp.arange(SPANWISE_SIZE, dtype=jnp.int32), SPANWISE_SIZE)[:, None, None] + eigen_wall(jnp.arange(VERTICAL_SIZE, dtype=jnp.int32), VERTICAL_SIZE)[None, :, None]
    positive = eigen_sum > 0
    solved = jnp.where(positive, -spectral / jnp.where(positive, eigen_sum, 1.0), 0.0)
    pressure = jnp.einsum('ykx,kz->yzx', solved, cosine_inverse(VERTICAL_SIZE), precision=lax.Precision.HIGHEST)
    pressure = hartley(pressure, 0) / SPANWISE_SIZE
    pressure = hartley(pressure, 2) / LENGTHWISE_SIZE
    grad_x = pressure - jnp.roll(pressure, 1, axis=2)
    grad_y = pressure - jnp.roll(pressure, 1, axis=0)
    below = jnp.concatenate([jnp.zeros((SPANWISE_SIZE, 1, LENGTHWISE_SIZE), jnp.float32), pressure[:, :-1]], 1)
    layer_index = jnp.arange(VERTICAL_SIZE, dtype=jnp.int32)
    grad_z = jnp.where((layer_index == 0)[None, :, None], 0.0, pressure - below)
    advanced_dual_motion = unprojected_motion - jnp.stack([grad_x, grad_y, grad_z])
    return advanced_dual_motion, advanced_dual_thermal
```

```python
import functools
import math

import jax
import jax.numpy as jnp
import ml_dtypes
import numpy as np
from jax import lax
from jax.experimental import pallas as pl
from jax.experimental.pallas import tpu as pltpu
from jax.sharding import PartitionSpec as P

time_step = 0.2
viscosity = 0.1
diffusivity = 0.1
buoyancy = 1.0
highest = lax.Precision.HIGHEST


def padded(cells, sides, width):
    for axis, dim in sides:
        count = lax.axis_size(axis)
        head = lax.slice_in_dim(cells, 0, width, axis=dim)
        tail = lax.slice_in_dim(cells, cells.shape[dim] - width, cells.shape[dim], axis=dim)
        cells = jnp.concatenate(
            [
                lax.ppermute(tail, axis, [(i, (i + 1) % count) for i in range(count)]),
                cells,
                lax.ppermute(head, axis, [((i + 1) % count, i) for i in range(count)]),
            ],
            axis=dim,
        )
    return cells


def shifted(value, axis, by):
    length = lax.axis_size(axis)
    return lax.ppermute(value, axis, [(i, (i + by) % length) for i in range(length)])


def from_behind(block, axis, distance):
    devices = range(lax.axis_size(axis))
    route = [(i - distance, i) for i in devices if i - distance in devices]
    return lax.ppermute(block, axis, route)


def tendency_contributions(haloed_quantities, motion_pieces):
    centre = haloed_quantities[:, 1:-1, 1:-1]
    slope_x = 0.5 * (jnp.roll(centre, -1, axis=3) - jnp.roll(centre, 1, axis=3))
    slope_y = 0.5 * (haloed_quantities[:, 2:, 1:-1] - haloed_quantities[:, :-2, 1:-1])
    slope_z = 0.5 * (haloed_quantities[:, 1:-1, 2:] - haloed_quantities[:, 1:-1, :-2])
    laplace = (
        jnp.roll(centre[:4], -1, axis=3)
        + jnp.roll(centre[:4], 1, axis=3)
        + (haloed_quantities[:4, 2:, 1:-1] + haloed_quantities[:4, :-2, 1:-1])
        + (haloed_quantities[:4, 1:-1, 2:] + haloed_quantities[:4, 1:-1, :-2])
        - 6.0 * centre[:4]
    )
    advect = (
        motion_pieces[0] * slope_x[:4]
        + motion_pieces[1] * slope_y[:4]
        + motion_pieces[2] * slope_z[:4]
    )
    heat_slope = jnp.stack([slope_x[4], slope_y[4], slope_z[4]])
    unprojected_motion = centre[:3] + time_step * (
        advect[:3] + viscosity * laplace[:3] + centre[3] * heat_slope
    )
    thermal_following = centre[3] + time_step * (
        advect[3] + diffusivity * laplace[3] + buoyancy * centre[2]
    )
    return (unprojected_motion, thermal_following)


def cas_table(length):
    indices = jnp.arange(length, dtype=jnp.int32)
    phases = indices[:, None] * indices[None, :] % length
    angles = phases.astype(jnp.float32) * (2.0 * math.pi / length)
    return jnp.cos(angles) + jnp.sin(angles)


def cosine_table(length):
    indices = jnp.arange(length, dtype=jnp.int32)
    phases = indices[None, :] * (2 * indices[:, None] + 1) % (4 * length)
    return jnp.cos(phases.astype(jnp.float32) * (math.pi / (2 * length)))


def cosine_inverse(length):
    indices = jnp.arange(length, dtype=jnp.int32)
    weights = jnp.where(indices == 0, 1.0, 2.0).astype(jnp.float32)
    return cosine_table(length).T * weights[:, None] / length


def eigen_periodic(waves, length):
    return 2.0 - 2.0 * jnp.cos(waves.astype(jnp.float32) * (2.0 * math.pi / length))


def eigen_wall(waves, length):
    return 2.0 - 2.0 * jnp.cos(waves.astype(jnp.float32) * (math.pi / length))


def invert(spectral, eigen_sum):
    positive = eigen_sum > 0
    return jnp.where(positive, -spectral / jnp.where(positive, eigen_sum, 1.0), 0.0)


def wall_mask(extent, margin, position, groups):
    layer_index = jnp.arange(extent, dtype=jnp.int32)
    bottom = (layer_index < margin) & (position == 0)
    ceiling = (layer_index >= extent - margin) & (position == groups - 1)
    return jnp.where(bottom | ceiling, 0.0, 1.0).astype(jnp.float32)


def poisson(source):
    spanwise_extent, vertical_extent, lengthwise_extent = source.shape
    groups_y = lax.axis_size("gy")
    groups_z = lax.axis_size("gz")
    span_y = spanwise_extent * groups_y
    span_z = vertical_extent * groups_z
    hart_x = cas_table(lengthwise_extent)
    hart_y = cas_table(span_y)
    cos_forward = cosine_table(span_z).reshape(groups_z, vertical_extent, span_z)
    cos_backward = cosine_inverse(span_z).reshape(span_z, groups_z, vertical_extent)
    line_z = eigen_wall(jnp.arange(span_z, dtype=jnp.int32), span_z)
    piece_x = lengthwise_extent // groups_y
    quarter = span_y // groups_z
    table_x = hart_x.reshape(lengthwise_extent, groups_y, piece_x)
    table_y = hart_y.reshape(groups_y, spanwise_extent, groups_z, quarter)
    step_one = jnp.einsum("yzx,xgj->gjyz", source, table_x, precision=highest).reshape(groups_y, -1)
    step_one = lax.all_to_all(step_one, "gy", split_axis=0, concat_axis=0, tiled=True).reshape(
        groups_y, piece_x, spanwise_extent, vertical_extent
    )
    step_two = jnp.einsum("sjyz,syhq->hjqz", step_one, table_y, precision=highest).reshape(
        groups_z, -1
    )
    step_two = lax.all_to_all(step_two, "gz", split_axis=0, concat_axis=0, tiled=True).reshape(
        groups_z, piece_x, quarter, vertical_extent
    )
    spectral = jnp.einsum("tjqc,tck->jqk", step_two, cos_forward, precision=highest)
    wave_x = lax.axis_index("gy") * piece_x + jnp.arange(piece_x, dtype=jnp.int32)
    wave_y = lax.axis_index("gz") * quarter + jnp.arange(quarter, dtype=jnp.int32)
    eigen_sum = (
        eigen_periodic(wave_x, lengthwise_extent)[:, None, None]
        + eigen_periodic(wave_y, span_y)[None, :, None]
        + line_z[None, None, :]
    )
    solved = invert(spectral, eigen_sum)
    step_three = jnp.einsum("jqk,ktc->tjqc", solved, cos_backward, precision=highest).reshape(
        groups_z, -1
    )
    step_three = lax.all_to_all(step_three, "gz", split_axis=0, concat_axis=0, tiled=True).reshape(
        groups_z, piece_x, quarter, vertical_extent
    )
    step_four = (
        jnp.einsum("hjqz,syhq->sjyz", step_three, table_y, precision=highest) * (1.0 / span_y)
    ).reshape(groups_y, -1)
    step_four = lax.all_to_all(step_four, "gy", split_axis=0, concat_axis=0, tiled=True).reshape(
        groups_y, piece_x, spanwise_extent, vertical_extent
    )
    return jnp.einsum("gjyz,xgj->yzx", step_four, table_x, precision=highest) * (
        1.0 / lengthwise_extent
    )


def on_device(dual_flow_speeds, dual_thermal_state, forward_flow_speeds, forward_thermal_state):
    spanwise_extent, vertical_extent, lengthwise_extent = dual_thermal_state.shape
    groups_z = lax.axis_size("gz")
    place_z = lax.axis_index("gz")
    motion_pieces = forward_flow_speeds.astype(jnp.float32)
    forward_thermal_flux = forward_thermal_state.astype(jnp.float32)
    stacked_fields = jnp.concatenate(
        [dual_flow_speeds, dual_thermal_state[None], forward_thermal_flux[None]], 0
    )
    haloed_quantities = padded(stacked_fields, (("gy", 1), ("gz", 2)), 1)
    haloed_quantities = (
        haloed_quantities
        * wall_mask(vertical_extent + 2, 1, place_z, groups_z)[None, None, :, None]
    )
    unprojected_motion, advanced_dual_thermal = tendency_contributions(
        haloed_quantities, motion_pieces
    )
    upper_y = shifted(unprojected_motion[1][0], "gy", -1)
    upper_z = from_behind(unprojected_motion[2][:, 0], "gz", -1)
    next_y = jnp.concatenate([unprojected_motion[1][1:], upper_y[None]], 0)
    next_z = jnp.concatenate([unprojected_motion[2][:, 1:], upper_z[:, None]], 1)
    source = (
        jnp.roll(unprojected_motion[0], -1, axis=2)
        - unprojected_motion[0]
        + (next_y - unprojected_motion[1])
        + (next_z - unprojected_motion[2])
    )
    pressure = poisson(source)
    grad_x = pressure - jnp.roll(pressure, 1, axis=2)
    lower_y = shifted(pressure[spanwise_extent - 1], "gy", 1)
    grad_y = pressure - jnp.concatenate([lower_y[None], pressure[:-1]], 0)
    lower_z = from_behind(pressure[:, vertical_extent - 1], "gz", 1)
    below = jnp.concatenate([lower_z[:, None], pressure[:, :-1]], 1)
    floor_layer = (jnp.arange(vertical_extent, dtype=jnp.int32) == 0) & (place_z == 0)
    grad_z = jnp.where(floor_layer[None, :, None], 0.0, pressure - below)
    advanced_dual_motion = unprojected_motion - jnp.stack([grad_x, grad_y, grad_z])
    return (advanced_dual_motion, advanced_dual_thermal)


def halves(table):
    high = table.astype(np.float32).astype(ml_dtypes.bfloat16)
    low = (table - high.astype(np.float64)).astype(np.float32).astype(ml_dtypes.bfloat16)
    return high, low


def cas_np(length):
    phases = np.outer(np.arange(length), np.arange(length)) % length
    angles = phases * (2.0 * np.pi / length)
    return np.cos(angles) + np.sin(angles)


@functools.lru_cache(maxsize=None)
def tables(length, span_y, span_z, groups_y, groups_z):
    hart_x = cas_np(length)
    chunks = groups_y // 2
    hx = [
        np.ascontiguousarray(t.reshape(length, chunks, length // chunks).transpose(1, 0, 2))
        for t in halves(hart_x)
    ]
    hart_y = cas_np(span_y)
    forward = halves(hart_y * (-1.0 / (span_y * length)))
    backward = halves(hart_y)
    ty = np.stack([np.concatenate([hi, hi, lo], 1) for hi, lo in (forward, backward)])
    line_x = 4.0 * np.sin(np.pi * np.arange(length) / length) ** 2
    line_y = 4.0 * np.sin(np.pi * np.arange(span_y) / span_y) ** 2
    modes = (line_x[None, :] + line_y[:, None]).astype(np.float32)
    modes = np.ascontiguousarray(modes.reshape(span_y, groups_y, -1).transpose(1, 0, 2))
    k = np.arange(span_z)
    basis = np.cos(np.pi * np.outer(k, 2 * k + 1) / (2 * span_z))
    eig = 4.0 * np.sin(np.pi * k / (2 * span_z)) ** 2
    scale = np.where(k == 0, 0.0, 2.0 / (span_z * np.where(k == 0, 1.0, eig)))
    mean_free = (basis.T * scale) @ basis
    mean_free = mean_free.astype(np.float32).reshape(groups_z, -1, span_z)
    return hx[0], hx[1], ty, modes, mean_free


def split_rows(value):
    high = value.astype(jnp.bfloat16)
    return high, (value - high.astype(jnp.float32)).astype(jnp.bfloat16)


def dot32(a, b):
    return jnp.dot(a, b, preferred_element_type=jnp.float32)


def fused_kernel(
    ny, nz, motion, thermal, flow, base, hx_hi, hx_lo, ty_in, modes_in, free_in,
    out_motion, out_thermal,
    F, U, TH, HH, HL, TY, LAM, FREE, ZS, ZR, P0, P1, P2, PZS, PZR, S, A, B, D, PHI,
    R, MSG, MR, A2, B2, PR, QZS, QZR, OM, OT, lsem, osem, hs, hr, as_, ar, bs, br, zs, zr,
):
    gy, gz = lax.axis_index("gy"), lax.axis_index("gz")
    rows, layers, length = thermal.shape
    mesh_id = pl.DeviceIdType.MESH
    up_y, down_y = (gy + 1) % ny, (gy + ny - 1) % ny
    has_up, has_down = gz < nz - 1, gz > 0

    loads = [
        pltpu.make_async_copy(motion, F.at[0:3, 1 : rows + 1], lsem.at[0]),
        pltpu.make_async_copy(thermal, F.at[3, 1 : rows + 1], lsem.at[1]),
        pltpu.make_async_copy(base, TH, lsem.at[2]),
        pltpu.make_async_copy(flow, U, lsem.at[3]),
        pltpu.make_async_copy(modes_in.at[gy], LAM, lsem.at[4]),
        pltpu.make_async_copy(free_in.at[gz], FREE, lsem.at[5]),
        pltpu.make_async_copy(ty_in, TY, lsem.at[6]),
        pltpu.make_async_copy(hx_hi, HH, lsem.at[7]),
        pltpu.make_async_copy(hx_lo, HL, lsem.at[8]),
    ]
    for copy in loads:
        copy.start()

    barrier = pltpu.get_barrier_semaphore()
    for i in range(1, ny):
        pl.semaphore_signal(
            barrier, inc=1, device_id=((gy + i) % ny, gz), device_id_type=mesh_id
        )
    for i in range(1, nz):
        pl.semaphore_signal(
            barrier, inc=1, device_id=(gy, (gz + i) % nz), device_id_type=mesh_id
        )

    def remote(src, dst, ssem, rsem, y, z):
        return pltpu.make_async_remote_copy(
            src_ref=src, dst_ref=dst, send_sem=ssem, recv_sem=rsem,
            device_id=(y, z), device_id_type=mesh_id,
        )

    loads[2].wait()
    for y in range(rows):
        F[4, y + 1] = TH[y].astype(jnp.float32)
    loads[0].wait()
    loads[1].wait()
    for f in range(5):
        for y in range(rows):
            ZS[0, f, y : y + 1, :] = F[f, y + 1, 0:1, :]
            ZS[1, f, y : y + 1, :] = F[f, y + 1, layers - 1 : layers, :]
    pl.semaphore_wait(barrier, ny + nz - 2)

    z_down = remote(ZS.at[0], ZR.at[1], hs.at[0], hr.at[0], gy, gz - 1)
    z_up = remote(ZS.at[1], ZR.at[0], hs.at[1], hr.at[1], gy, gz + 1)
    y_down = remote(F.at[:, 1], F.at[:, rows + 1], hs.at[2], hr.at[2], down_y, gz)
    y_up = remote(F.at[:, rows], F.at[:, 0], hs.at[3], hr.at[3], up_y, gz)

    @pl.when(has_down)
    def _():
        z_down.start()

    @pl.when(has_up)
    def _():
        z_up.start()

    y_down.start()
    y_up.start()

    @pl.when(gz == 0)
    def _():
        ZR[0] = jnp.zeros_like(ZR[0])

    @pl.when(gz == nz - 1)
    def _():
        ZR[1] = jnp.zeros_like(ZR[1])
        PZR[...] = jnp.zeros_like(PZR)

    loads[4].wait()
    D[0] = jnp.zeros_like(D[0])

    def ratios(block, carry):
        def one(i, prod):
            at = block * layers + i
            e = LAM[...] + D[at]
            d = e / (1.0 + e)
            D[at + 1] = d
            return prod * (1.0 - d)

        PHI[block] = lax.fori_loop(0, layers, one, jnp.ones_like(LAM[...]))
        return carry

    lax.fori_loop(0, nz, ratios, 0)

    loads[3].wait()

    @pl.when(has_up)
    def _():
        z_down.wait_recv()

    @pl.when(has_down)
    def _():
        z_up.wait_recv()

    y_down.wait_recv()
    y_up.wait_recv()

    zi = lax.broadcasted_iota(jnp.int32, (layers, length), 0)

    def stencil(y, carry):
        def sides(f):
            c = F[f, y + 1]
            xp, xm = pltpu.roll(c, length - 1, 1), pltpu.roll(c, 1, 1)
            zp = jnp.where(zi == layers - 1, ZR[1, f, pl.ds(y, 1), :], pltpu.roll(c, layers - 1, 0))
            zm = jnp.where(zi == 0, ZR[0, f, pl.ds(y, 1), :], pltpu.roll(c, 1, 0))
            return c, xp, xm, F[f, y + 2], F[f, y], zp, zm

        u0, u1, u2 = (U[d, y].astype(jnp.float32) for d in range(3))

        def advance(f):
            c, xp, xm, yp, ym, zp, zm = sides(f)
            adv = 0.5 * (u0 * (xp - xm) + u1 * (yp - ym) + u2 * (zp - zm))
            lap = (xp + xm) + (yp + ym) + (zp + zm) - 6.0 * c
            return c, adv + viscosity * lap

        c3, t3 = advance(3)
        _, hxp, hxm, hyp, hym, hzp, hzm = sides(4)
        half = 0.5 * c3
        c, t = advance(0)
        P0[y] = c + time_step * (t + half * (hxp - hxm))
        c, t = advance(1)
        P1[y] = c + time_step * (t + half * (hyp - hym))
        c, t = advance(2)
        p2 = c + time_step * (t + half * (hzp - hzm))
        P2[y] = p2
        PZS[pl.ds(y, 1), :] = p2[0:1, :]
        OT[y] = c3 + time_step * (t3 + buoyancy * c)
        return carry

    p1_down = remote(P1.at[0], P1.at[rows], hs.at[4], hr.at[4], down_y, gz)
    p2_down = remote(PZS, PZR, hs.at[5], hr.at[5], gy, gz - 1)
    stencil(0, 0)
    p1_down.start()
    lax.fori_loop(1, rows, stencil, 0)

    @pl.when(has_down)
    def _():
        p2_down.start()

    out_t = pltpu.make_async_copy(OT, out_thermal, osem.at[0])
    out_t.start()

    @pl.when(has_up)
    def _():
        p2_down.wait_recv()

    p1_down.wait_recv()
    half_rows = rows * layers

    def diverge(y, carry):
        p0, p2 = P0[y], P2[y]
        zp = jnp.where(zi == layers - 1, PZR[pl.ds(y, 1), :], pltpu.roll(p2, layers - 1, 0))
        s = (pltpu.roll(p0, length - 1, 1) - p0) + (P1[y + 1] - P1[y]) + (zp - p2)
        high, low = split_rows(s)
        S[pl.ds(pl.multiple_of(y * layers, layers), layers), :] = high
        S[pl.ds(pl.multiple_of(half_rows + y * layers, layers), layers), :] = low
        return carry

    lax.fori_loop(0, rows, diverge, 0)

    loads[7].wait()
    loads[8].wait()
    chunks = ny // 2

    def x_forward(i, carry):
        c = (gy // 2 + 1 + i) % chunks
        wide = dot32(S[...], HH[c])
        part = wide[:half_rows] + wide[half_rows:] + dot32(S[0:half_rows, :], HL[c])
        for side in range(2):
            peer = 2 * c + side
            A[peer] = part[:, side * 128 : (side + 1) * 128]

            @pl.when(peer != gy)
            def _():
                remote(A.at[peer], B.at[gy], as_.at[peer], ar.at[gy], peer, gz).start()

            @pl.when(peer == gy)
            def _():
                B[peer] = A[peer]

        return carry

    lax.fori_loop(0, chunks, x_forward, 0)
    loads[5].wait()
    loads[6].wait()

    def wait_all(src, dst, ssem, rsem):
        def one(i, carry):
            peer = (gy + i) % ny
            remote(src.at[peer], dst.at[peer], ssem.at[peer], rsem.at[peer], peer, gz).wait_recv()
            return carry

        lax.fori_loop(1, ny, one, 0)

    wait_all(A, B, as_, ar)
    span_y = ny * rows
    flat = B.reshape(ny * half_rows, 128)

    def y_transform(pair, table):
        high, low = split_rows(pair)
        return dot32(table, jnp.concatenate([high, low, high], 0))

    f_sweep = None
    start = gz * layers
    total = nz * layers
    for z in range(0, layers, 2):
        pair = jnp.concatenate(
            [flat[pl.ds(z + k, span_y, stride=layers), :] for k in range(2)], 1
        )
        res = y_transform(pair, TY[0])
        for k in range(2):
            r = res[:, k * 128 : (k + 1) * 128]
            R[z + k] = r
            MSG[0, span_y + z + k : span_y + z + k + 1, :] = r[0:1, :]
            MSG[1, span_y + z + k : span_y + z + k + 1, :] = r[0:1, :]
            w = 1.0 - D[start + z + k + 1]
            f_sweep = w * (r if f_sweep is None else r + f_sweep)
    MSG[0, 0:span_y, :] = f_sweep
    g_sweep = jnp.zeros_like(f_sweep)
    for z in range(layers - 1, -1, -1):
        g_sweep = (1.0 - D[total - start - z]) * (R[z] + g_sweep)
    MSG[1, 0:span_y, :] = g_sweep

    for i in range(1, nz):
        peer = (gz + i) % nz

        @pl.when(peer > gz)
        def _():
            remote(MSG.at[0], MR.at[gz], zs.at[peer], zr.at[gz], gy, peer).start()

        @pl.when(peer < gz)
        def _():
            remote(MSG.at[1], MR.at[gz], zs.at[peer], zr.at[gz], gy, peer).start()

    MR[gz] = MSG[0]
    for i in range(1, nz):
        peer = (gz + i) % nz
        remote(MSG.at[0], MR.at[peer], zs.at[peer], zr.at[peer], gy, peer).wait_recv()

    f = jnp.zeros_like(f_sweep)
    g = jnp.zeros_like(f_sweep)
    for s in range(nz):
        f = jnp.where(s < gz, MR[s, 0:span_y, :] + PHI[s] * f, f)
    for s in range(nz - 1, -1, -1):
        g = jnp.where(s > gz, MR[s, 0:span_y, :] + PHI[nz - 1 - s] * g, g)
    line = jnp.concatenate([MR[s, span_y:, :] for s in range(nz)], 0)
    level = jnp.dot(FREE[...], line, precision=highest, preferred_element_type=jnp.float32)
    plain = LAM[...] > 0.0
    for z in range(layers):
        f = (1.0 - D[start + z + 1]) * (R[z] + f)
        R[z] = f
    d_low, d_high = D[start + layers], D[total - start - layers]
    below = d_low + d_high - d_low * d_high
    p = (f + (1.0 - d_low) * g) / jnp.where(plain, below, 1.0)
    R[layers - 1] = p
    for z in range(layers - 2, -1, -1):
        p = (1.0 - D[start + z + 1]) * p + R[z]
        R[z] = p
    flat2 = A2.reshape(ny * half_rows, 128)
    for z in range(0, layers, 2):
        pair = jnp.concatenate(
            [jnp.where(plain, R[z + k], level[z + k : z + k + 1, :]) for k in range(2)], 1
        )
        res = y_transform(pair, TY[1])
        for k in range(2):
            flat2[pl.ds(z + k, span_y, stride=layers), :] = res[:, k * 128 : (k + 1) * 128]

    def send_back(i, carry):
        peer = (gy + i) % ny
        remote(A2.at[peer], B2.at[gy], bs.at[peer], br.at[gy], peer, gz).start()
        return carry

    lax.fori_loop(1, ny, send_back, 0)
    B2[gy] = A2[gy]
    wait_all(A2, B2, bs, br)

    q = jnp.concatenate([B2[s] for s in range(ny)], 1)
    high, low = split_rows(q)
    S[0:half_rows, :] = high
    S[half_rows:, :] = low
    width = length // chunks
    for c in range(chunks):
        wide = dot32(S[...], HH[c])
        part = wide[:half_rows] + wide[half_rows:] + dot32(S[0:half_rows, :], HL[c])
        PR[1 : rows + 1, :, c * width : (c + 1) * width] = part.reshape(rows, layers, width)
    pr_up = remote(PR.at[rows], PR.at[0], hs.at[6], hr.at[6], up_y, gz)
    pz_up = remote(QZS, QZR, hs.at[7], hr.at[7], gy, gz + 1)
    pr_up.start()
    for y in range(rows):
        QZS[y : y + 1, :] = PR[y + 1, layers - 1 : layers, :]

    @pl.when(has_up)
    def _():
        pz_up.start()

    @pl.when(gz == 0)
    def _():
        for y in range(rows):
            QZR[y : y + 1, :] = PR[y + 1, 0:1, :]

    @pl.when(has_down)
    def _():
        pz_up.wait_recv()

    pr_up.wait_recv()

    def project(y, carry):
        p = PR[y + 1]
        zm = jnp.where(zi == 0, QZR[pl.ds(y, 1), :], pltpu.roll(p, 1, 0))
        OM[0, y] = P0[y] - (p - pltpu.roll(p, 1, 1))
        OM[1, y] = P1[y] - (p - PR[y])
        OM[2, y] = P2[y] - (p - zm)
        return carry

    lax.fori_loop(0, rows, project, 0)
    out_m = pltpu.make_async_copy(OM, out_motion, osem.at[1])
    out_m.start()

    @pl.when(has_down)
    def _():
        z_down.wait_send()
        p2_down.wait_send()

    @pl.when(has_up)
    def _():
        z_up.wait_send()
        pz_up.wait_send()

    for copy in (y_down, y_up, p1_down, pr_up):
        copy.wait_send()

    def finish(i, carry):
        peer = (gy + i) % ny
        remote(A.at[peer], B.at[gy], as_.at[peer], ar.at[gy], peer, gz).wait_send()
        remote(A2.at[peer], B2.at[gy], bs.at[peer], br.at[gy], peer, gz).wait_send()
        return carry

    lax.fori_loop(1, ny, finish, 0)
    for i in range(1, nz):
        peer = (gz + i) % nz
        remote(MSG.at[0], MR.at[gz], zs.at[peer], zr.at[gz], gy, peer).wait_send()
    out_t.wait()
    out_m.wait()


def fused_step(ny, nz, motion, thermal, flow, base):
    rows, layers, length = thermal.shape
    span_y, span_z = ny * rows, nz * layers
    constants = [jnp.asarray(t) for t in tables(length, span_y, span_z, ny, nz)]
    f32, b16 = jnp.float32, jnp.bfloat16
    flat = rows * layers
    vmem, dma = pltpu.VMEM, pltpu.SemaphoreType.DMA
    scratch = [
        vmem((5, rows + 2, layers, length), f32),
        vmem(flow.shape, b16),
        vmem(base.shape, b16),
        vmem(constants[0].shape, b16),
        vmem(constants[1].shape, b16),
        vmem(constants[2].shape, b16),
        vmem((span_y, 128), f32),
        vmem((layers, span_z), f32),
        vmem((2, 5, rows, length), f32),
        vmem((2, 5, rows, length), f32),
        vmem((rows, layers, length), f32),
        vmem((rows + 1, layers, length), f32),
        vmem((rows, layers, length), f32),
        vmem((rows, length), f32),
        vmem((rows, length), f32),
        vmem((2 * flat, length), b16),
        vmem((ny, flat, 128), f32),
        vmem((ny, flat, 128), f32),
        vmem((span_z + 1, span_y, 128), f32),
        vmem((nz, span_y, 128), f32),
        vmem((layers, span_y, 128), f32),
        vmem((2, span_y + layers, 128), f32),
        vmem((nz, span_y + layers, 128), f32),
        vmem((ny, flat, 128), f32),
        vmem((ny, flat, 128), f32),
        vmem((rows + 1, layers, length), f32),
        vmem((rows, length), f32),
        vmem((rows, length), f32),
        vmem((3, rows, layers, length), f32),
        vmem((rows, layers, length), f32),
        dma((9,)),
        dma((2,)),
        dma((8,)),
        dma((8,)),
        dma((ny,)),
        dma((ny,)),
        dma((ny,)),
        dma((ny,)),
        dma((nz,)),
        dma((nz,)),
    ]
    hbm = pl.BlockSpec(memory_space=pl.ANY)
    return pl.pallas_call(
        functools.partial(fused_kernel, ny, nz),
        out_shape=(
            jax.ShapeDtypeStruct(motion.shape, f32),
            jax.ShapeDtypeStruct(thermal.shape, f32),
        ),
        in_specs=[hbm] * 9,
        out_specs=(hbm, hbm),
        scratch_shapes=scratch,
        compiler_params=pltpu.CompilerParams(
            collective_id=0, has_side_effects=True, vmem_limit_bytes=44 * 2**20
        ),
        cost_estimate=pl.CostEstimate(
            flops=12 * flat * length * length, bytes_accessed=10 * 2**20, transcendentals=0
        ),
    )(motion, thermal, flow, base, *constants)


def solution(mesh):
    placed = (
        P(None, "gy", "gz", None),
        P("gy", "gz", None),
        P(None, "gy", "gz", None),
        P("gy", "gz", None),
    )
    groups_y, groups_z = mesh.shape["gy"], mesh.shape["gz"]

    def step(motion, thermal, flow, base):
        rows, layers, length = thermal.shape
        if length == 128 * groups_y and groups_y % 2 == 0 and rows == 8 and layers == 16:
            return fused_step(groups_y, groups_z, motion, thermal, flow, base)
        return on_device(motion, thermal, flow, base)

    return jax.shard_map(
        step,
        mesh=mesh,
        in_specs=placed,
        out_specs=(P(None, "gy", "gz", None), P("gy", "gz", None)),
        check_vma=False,
    )
```

```python
import functools
import math

import jax
import jax.numpy as jnp
import ml_dtypes
import numpy as np
from jax import lax
from jax.experimental import pallas as pl
from jax.experimental.pallas import tpu as pltpu
from jax.sharding import PartitionSpec as P

time_step = 0.2
viscosity = 0.1
diffusivity = 0.1
buoyancy = 1.0
highest = lax.Precision.HIGHEST


def padded(cells, sides, width):
    for axis, dim in sides:
        count = lax.axis_size(axis)
        head = lax.slice_in_dim(cells, 0, width, axis=dim)
        tail = lax.slice_in_dim(cells, cells.shape[dim] - width, cells.shape[dim], axis=dim)
        cells = jnp.concatenate(
            [
                lax.ppermute(tail, axis, [(i, (i + 1) % count) for i in range(count)]),
                cells,
                lax.ppermute(head, axis, [((i + 1) % count, i) for i in range(count)]),
            ],
            axis=dim,
        )
    return cells


def shifted(value, axis, by):
    length = lax.axis_size(axis)
    return lax.ppermute(value, axis, [(i, (i + by) % length) for i in range(length)])


def from_behind(block, axis, distance):
    devices = range(lax.axis_size(axis))
    route = [(i - distance, i) for i in devices if i - distance in devices]
    return lax.ppermute(block, axis, route)


def tendency_contributions(haloed_quantities, motion_pieces):
    centre = haloed_quantities[:, 1:-1, 1:-1]
    slope_x = 0.5 * (jnp.roll(centre, -1, axis=3) - jnp.roll(centre, 1, axis=3))
    slope_y = 0.5 * (haloed_quantities[:, 2:, 1:-1] - haloed_quantities[:, :-2, 1:-1])
    slope_z = 0.5 * (haloed_quantities[:, 1:-1, 2:] - haloed_quantities[:, 1:-1, :-2])
    laplace = (
        jnp.roll(centre[:4], -1, axis=3)
        + jnp.roll(centre[:4], 1, axis=3)
        + (haloed_quantities[:4, 2:, 1:-1] + haloed_quantities[:4, :-2, 1:-1])
        + (haloed_quantities[:4, 1:-1, 2:] + haloed_quantities[:4, 1:-1, :-2])
        - 6.0 * centre[:4]
    )
    advect = (
        motion_pieces[0] * slope_x[:4]
        + motion_pieces[1] * slope_y[:4]
        + motion_pieces[2] * slope_z[:4]
    )
    heat_slope = jnp.stack([slope_x[4], slope_y[4], slope_z[4]])
    unprojected_motion = centre[:3] + time_step * (
        advect[:3] + viscosity * laplace[:3] + centre[3] * heat_slope
    )
    thermal_following = centre[3] + time_step * (
        advect[3] + diffusivity * laplace[3] + buoyancy * centre[2]
    )
    return (unprojected_motion, thermal_following)


def cas_table(length):
    indices = jnp.arange(length, dtype=jnp.int32)
    phases = indices[:, None] * indices[None, :] % length
    angles = phases.astype(jnp.float32) * (2.0 * math.pi / length)
    return jnp.cos(angles) + jnp.sin(angles)


def cosine_table(length):
    indices = jnp.arange(length, dtype=jnp.int32)
    phases = indices[None, :] * (2 * indices[:, None] + 1) % (4 * length)
    return jnp.cos(phases.astype(jnp.float32) * (math.pi / (2 * length)))


def cosine_inverse(length):
    indices = jnp.arange(length, dtype=jnp.int32)
    weights = jnp.where(indices == 0, 1.0, 2.0).astype(jnp.float32)
    return cosine_table(length).T * weights[:, None] / length


def eigen_periodic(waves, length):
    return 2.0 - 2.0 * jnp.cos(waves.astype(jnp.float32) * (2.0 * math.pi / length))


def eigen_wall(waves, length):
    return 2.0 - 2.0 * jnp.cos(waves.astype(jnp.float32) * (math.pi / length))


def invert(spectral, eigen_sum):
    positive = eigen_sum > 0
    return jnp.where(positive, -spectral / jnp.where(positive, eigen_sum, 1.0), 0.0)


def wall_mask(extent, margin, position, groups):
    layer_index = jnp.arange(extent, dtype=jnp.int32)
    bottom = (layer_index < margin) & (position == 0)
    ceiling = (layer_index >= extent - margin) & (position == groups - 1)
    return jnp.where(bottom | ceiling, 0.0, 1.0).astype(jnp.float32)


def poisson(source):
    spanwise_extent, vertical_extent, lengthwise_extent = source.shape
    groups_y = lax.axis_size("gy")
    groups_z = lax.axis_size("gz")
    span_y = spanwise_extent * groups_y
    span_z = vertical_extent * groups_z
    hart_x = cas_table(lengthwise_extent)
    hart_y = cas_table(span_y)
    cos_forward = cosine_table(span_z).reshape(groups_z, vertical_extent, span_z)
    cos_backward = cosine_inverse(span_z).reshape(span_z, groups_z, vertical_extent)
    line_z = eigen_wall(jnp.arange(span_z, dtype=jnp.int32), span_z)
    piece_x = lengthwise_extent // groups_y
    quarter = span_y // groups_z
    table_x = hart_x.reshape(lengthwise_extent, groups_y, piece_x)
    table_y = hart_y.reshape(groups_y, spanwise_extent, groups_z, quarter)
    step_one = jnp.einsum("yzx,xgj->gjyz", source, table_x, precision=highest).reshape(groups_y, -1)
    step_one = lax.all_to_all(step_one, "gy", split_axis=0, concat_axis=0, tiled=True).reshape(
        groups_y, piece_x, spanwise_extent, vertical_extent
    )
    step_two = jnp.einsum("sjyz,syhq->hjqz", step_one, table_y, precision=highest).reshape(
        groups_z, -1
    )
    step_two = lax.all_to_all(step_two, "gz", split_axis=0, concat_axis=0, tiled=True).reshape(
        groups_z, piece_x, quarter, vertical_extent
    )
    spectral = jnp.einsum("tjqc,tck->jqk", step_two, cos_forward, precision=highest)
    wave_x = lax.axis_index("gy") * piece_x + jnp.arange(piece_x, dtype=jnp.int32)
    wave_y = lax.axis_index("gz") * quarter + jnp.arange(quarter, dtype=jnp.int32)
    eigen_sum = (
        eigen_periodic(wave_x, lengthwise_extent)[:, None, None]
        + eigen_periodic(wave_y, span_y)[None, :, None]
        + line_z[None, None, :]
    )
    solved = invert(spectral, eigen_sum)
    step_three = jnp.einsum("jqk,ktc->tjqc", solved, cos_backward, precision=highest).reshape(
        groups_z, -1
    )
    step_three = lax.all_to_all(step_three, "gz", split_axis=0, concat_axis=0, tiled=True).reshape(
        groups_z, piece_x, quarter, vertical_extent
    )
    step_four = (
        jnp.einsum("hjqz,syhq->sjyz", step_three, table_y, precision=highest) * (1.0 / span_y)
    ).reshape(groups_y, -1)
    step_four = lax.all_to_all(step_four, "gy", split_axis=0, concat_axis=0, tiled=True).reshape(
        groups_y, piece_x, spanwise_extent, vertical_extent
    )
    return jnp.einsum("gjyz,xgj->yzx", step_four, table_x, precision=highest) * (
        1.0 / lengthwise_extent
    )


def on_device(dual_flow_speeds, dual_thermal_state, forward_flow_speeds, forward_thermal_state):
    spanwise_extent, vertical_extent, lengthwise_extent = dual_thermal_state.shape
    groups_z = lax.axis_size("gz")
    place_z = lax.axis_index("gz")
    motion_pieces = forward_flow_speeds.astype(jnp.float32)
    forward_thermal_flux = forward_thermal_state.astype(jnp.float32)
    stacked_fields = jnp.concatenate(
        [dual_flow_speeds, dual_thermal_state[None], forward_thermal_flux[None]], 0
    )
    haloed_quantities = padded(stacked_fields, (("gy", 1), ("gz", 2)), 1)
    haloed_quantities = (
        haloed_quantities
        * wall_mask(vertical_extent + 2, 1, place_z, groups_z)[None, None, :, None]
    )
    unprojected_motion, advanced_dual_thermal = tendency_contributions(
        haloed_quantities, motion_pieces
    )
    upper_y = shifted(unprojected_motion[1][0], "gy", -1)
    upper_z = from_behind(unprojected_motion[2][:, 0], "gz", -1)
    next_y = jnp.concatenate([unprojected_motion[1][1:], upper_y[None]], 0)
    next_z = jnp.concatenate([unprojected_motion[2][:, 1:], upper_z[:, None]], 1)
    source = (
        jnp.roll(unprojected_motion[0], -1, axis=2)
        - unprojected_motion[0]
        + (next_y - unprojected_motion[1])
        + (next_z - unprojected_motion[2])
    )
    pressure = poisson(source)
    grad_x = pressure - jnp.roll(pressure, 1, axis=2)
    lower_y = shifted(pressure[spanwise_extent - 1], "gy", 1)
    grad_y = pressure - jnp.concatenate([lower_y[None], pressure[:-1]], 0)
    lower_z = from_behind(pressure[:, vertical_extent - 1], "gz", 1)
    below = jnp.concatenate([lower_z[:, None], pressure[:, :-1]], 1)
    floor_layer = (jnp.arange(vertical_extent, dtype=jnp.int32) == 0) & (place_z == 0)
    grad_z = jnp.where(floor_layer[None, :, None], 0.0, pressure - below)
    advanced_dual_motion = unprojected_motion - jnp.stack([grad_x, grad_y, grad_z])
    return (advanced_dual_motion, advanced_dual_thermal)


def halves(table):
    high = table.astype(np.float32).astype(ml_dtypes.bfloat16)
    low = (table - high.astype(np.float64)).astype(np.float32).astype(ml_dtypes.bfloat16)
    return high, low


def cas_np(length):
    phases = np.outer(np.arange(length), np.arange(length)) % length
    angles = phases * (2.0 * np.pi / length)
    return np.cos(angles) + np.sin(angles)


@functools.lru_cache(maxsize=None)
def tables(length, span_y, span_z, groups_y, groups_z):
    hart_x = cas_np(length)
    chunks = groups_y // 2
    hx = [
        np.ascontiguousarray(t.reshape(length, chunks, length // chunks).transpose(1, 0, 2))
        for t in halves(hart_x)
    ]
    hart_y = cas_np(span_y)
    forward = halves(hart_y * (-1.0 / (span_y * length)))
    backward = halves(hart_y)
    ty = np.stack([np.concatenate([hi, hi, lo], 1) for hi, lo in (forward, backward)])
    line_x = 4.0 * np.sin(np.pi * np.arange(length) / length) ** 2
    line_y = 4.0 * np.sin(np.pi * np.arange(span_y) / span_y) ** 2
    modes = (line_x[None, :] + line_y[:, None]).astype(np.float32)
    modes = np.ascontiguousarray(modes.reshape(span_y, groups_y, -1).transpose(1, 0, 2))
    k = np.arange(span_z)
    basis = np.cos(np.pi * np.outer(k, 2 * k + 1) / (2 * span_z))
    eig = 4.0 * np.sin(np.pi * k / (2 * span_z)) ** 2
    scale = np.where(k == 0, 0.0, 2.0 / (span_z * np.where(k == 0, 1.0, eig)))
    mean_free = (basis.T * scale) @ basis
    mean_free = mean_free.astype(np.float32).reshape(groups_z, -1, span_z)
    return hx[0], hx[1], ty, modes, mean_free


def split_rows(value):
    high = value.astype(jnp.bfloat16)
    return high, (value - high.astype(jnp.float32)).astype(jnp.bfloat16)


def dot32(a, b):
    return jnp.dot(a, b, preferred_element_type=jnp.float32)


def fused_kernel(
    ny, nz, motion, thermal, flow, base, hx_hi, hx_lo, ty_in, modes_in, free_in,
    OM, OT,
    F, U, TH, HH, HL, TY, LAM, FREE, ZS, ZR, P0, P1, P2, PZS, PZR, S, A, B, D, PHI,
    R, MSG, MR, A2, B2, PR, QZS, QZR, lsem, hs, hr, as_, ar, bs, br, zs, zr,
):
    gy, gz = lax.axis_index("gy"), lax.axis_index("gz")
    rows, layers, length = thermal.shape
    mesh_id = pl.DeviceIdType.MESH
    up_y, down_y = (gy + 1) % ny, (gy + ny - 1) % ny
    has_up, has_down = gz < nz - 1, gz > 0

    loads = [
        pltpu.make_async_copy(motion, F.at[0:3, 1 : rows + 1], lsem.at[0]),
        pltpu.make_async_copy(thermal, F.at[3, 1 : rows + 1], lsem.at[1]),
        pltpu.make_async_copy(base, TH, lsem.at[2]),
        pltpu.make_async_copy(flow, U, lsem.at[3]),
        pltpu.make_async_copy(modes_in.at[gy], LAM, lsem.at[4]),
        pltpu.make_async_copy(free_in.at[gz], FREE, lsem.at[5]),
        pltpu.make_async_copy(ty_in, TY, lsem.at[6]),
        pltpu.make_async_copy(hx_hi, HH, lsem.at[7]),
        pltpu.make_async_copy(hx_lo, HL, lsem.at[8]),
    ]
    for copy in loads:
        copy.start()

    barrier = pltpu.get_barrier_semaphore()
    for i in range(1, ny):
        pl.semaphore_signal(
            barrier, inc=1, device_id=((gy + i) % ny, gz), device_id_type=mesh_id
        )
    for i in range(1, nz):
        pl.semaphore_signal(
            barrier, inc=1, device_id=(gy, (gz + i) % nz), device_id_type=mesh_id
        )

    def remote(src, dst, ssem, rsem, y, z):
        return pltpu.make_async_remote_copy(
            src_ref=src, dst_ref=dst, send_sem=ssem, recv_sem=rsem,
            device_id=(y, z), device_id_type=mesh_id,
        )

    loads[2].wait()
    for y in range(rows):
        F[4, y + 1] = TH[y].astype(jnp.float32)
    loads[0].wait()
    loads[1].wait()
    for f in range(5):
        for y in range(rows):
            ZS[0, f, y : y + 1, :] = F[f, y + 1, 0:1, :]
            ZS[1, f, y : y + 1, :] = F[f, y + 1, layers - 1 : layers, :]
    pl.semaphore_wait(barrier, ny + nz - 2)

    z_down = remote(ZS.at[0], ZR.at[1], hs.at[0], hr.at[0], gy, gz - 1)
    z_up = remote(ZS.at[1], ZR.at[0], hs.at[1], hr.at[1], gy, gz + 1)
    y_down = remote(F.at[:, 1], F.at[:, rows + 1], hs.at[2], hr.at[2], down_y, gz)
    y_up = remote(F.at[:, rows], F.at[:, 0], hs.at[3], hr.at[3], up_y, gz)

    @pl.when(has_down)
    def _():
        z_down.start()

    @pl.when(has_up)
    def _():
        z_up.start()

    y_down.start()
    y_up.start()

    @pl.when(gz == 0)
    def _():
        ZR[0] = jnp.zeros_like(ZR[0])

    @pl.when(gz == nz - 1)
    def _():
        ZR[1] = jnp.zeros_like(ZR[1])
        PZR[...] = jnp.zeros_like(PZR)

    loads[4].wait()
    D[0] = jnp.zeros_like(D[0])

    def ratios(block, carry):
        def one(i, prod):
            at = block * layers + i
            e = LAM[...] + D[at]
            d = e / (1.0 + e)
            D[at + 1] = d
            return prod * (1.0 - d)

        PHI[block] = lax.fori_loop(0, layers, one, jnp.ones_like(LAM[...]))
        return carry

    lax.fori_loop(0, nz, ratios, 0)

    loads[3].wait()

    @pl.when(has_up)
    def _():
        z_down.wait_recv()

    @pl.when(has_down)
    def _():
        z_up.wait_recv()

    zi = lax.broadcasted_iota(jnp.int32, (layers, length), 0)

    def stencil(y, carry):
        def sides(f):
            c = F[f, y + 1]
            xp, xm = pltpu.roll(c, length - 1, 1), pltpu.roll(c, 1, 1)
            zp = jnp.where(zi == layers - 1, ZR[1, f, pl.ds(y, 1), :], pltpu.roll(c, layers - 1, 0))
            zm = jnp.where(zi == 0, ZR[0, f, pl.ds(y, 1), :], pltpu.roll(c, 1, 0))
            return c, xp, xm, F[f, y + 2], F[f, y], zp, zm

        u0, u1, u2 = (U[d, y].astype(jnp.float32) for d in range(3))

        def advance(f):
            c, xp, xm, yp, ym, zp, zm = sides(f)
            adv = 0.5 * (u0 * (xp - xm) + u1 * (yp - ym) + u2 * (zp - zm))
            lap = (xp + xm) + (yp + ym) + (zp + zm) - 6.0 * c
            return c, adv + viscosity * lap

        c3, t3 = advance(3)
        _, hxp, hxm, hyp, hym, hzp, hzm = sides(4)
        half = 0.5 * c3
        c, t = advance(0)
        P0[y] = c + time_step * (t + half * (hxp - hxm))
        c, t = advance(1)
        P1[y] = c + time_step * (t + half * (hyp - hym))
        c, t = advance(2)
        p2 = c + time_step * (t + half * (hzp - hzm))
        P2[y] = p2
        PZS[pl.ds(y, 1), :] = p2[0:1, :]
        OT[y] = c3 + time_step * (t3 + buoyancy * c)
        return carry

    p1_down = remote(P1.at[0], P1.at[rows], hs.at[4], hr.at[4], down_y, gz)
    p2_down = remote(PZS, PZR, hs.at[5], hr.at[5], gy, gz - 1)
    lax.fori_loop(1, rows - 1, stencil, 0)
    y_down.wait_recv()
    y_up.wait_recv()
    stencil(0, 0)
    p1_down.start()
    stencil(rows - 1, 0)

    @pl.when(has_down)
    def _():
        p2_down.start()

    @pl.when(has_up)
    def _():
        p2_down.wait_recv()

    p1_down.wait_recv()
    half_rows = rows * layers

    def diverge(y, carry):
        p0, p2 = P0[y], P2[y]
        zp = jnp.where(zi == layers - 1, PZR[pl.ds(y, 1), :], pltpu.roll(p2, layers - 1, 0))
        s = (pltpu.roll(p0, length - 1, 1) - p0) + (P1[y + 1] - P1[y]) + (zp - p2)
        high, low = split_rows(s)
        S[pl.ds(pl.multiple_of(y * layers, layers), layers), :] = high
        S[pl.ds(pl.multiple_of(half_rows + y * layers, layers), layers), :] = low
        return carry

    lax.fori_loop(0, rows, diverge, 0)

    loads[7].wait()
    loads[8].wait()
    chunks = ny // 2

    def x_forward(i, carry):
        c = (gy // 2 + 1 + i) % chunks
        wide = dot32(S[...], HH[c])
        part = wide[:half_rows] + wide[half_rows:] + dot32(S[0:half_rows, :], HL[c])
        for side in range(2):
            peer = 2 * c + side
            A[peer] = part[:, side * 128 : (side + 1) * 128]

            @pl.when(peer != gy)
            def _():
                remote(A.at[peer], B.at[gy], as_.at[peer], ar.at[gy], peer, gz).start()

            @pl.when(peer == gy)
            def _():
                B[peer] = A[peer]

        return carry

    lax.fori_loop(0, chunks, x_forward, 0)
    loads[5].wait()
    loads[6].wait()

    def wait_all(src, dst, ssem, rsem):
        def one(i, carry):
            peer = (gy + i) % ny
            remote(src.at[peer], dst.at[peer], ssem.at[peer], rsem.at[peer], peer, gz).wait_recv()
            return carry

        lax.fori_loop(1, ny, one, 0)

    wait_all(A, B, as_, ar)
    span_y = ny * rows
    flat = B.reshape(ny * half_rows, 128)

    def y_transform(pair, table):
        high, low = split_rows(pair)
        return dot32(table, jnp.concatenate([high, low, high], 0))

    f_sweep = None
    start = gz * layers
    total = nz * layers
    for z in range(0, layers, 2):
        pair = jnp.concatenate(
            [flat[pl.ds(z + k, span_y, stride=layers), :] for k in range(2)], 1
        )
        res = y_transform(pair, TY[0])
        for k in range(2):
            r = res[:, k * 128 : (k + 1) * 128]
            R[z + k] = r
            MSG[0, span_y + z + k : span_y + z + k + 1, :] = r[0:1, :]
            MSG[1, span_y + z + k : span_y + z + k + 1, :] = r[0:1, :]
            w = 1.0 - D[start + z + k + 1]
            f_sweep = w * (r if f_sweep is None else r + f_sweep)
    MSG[0, 0:span_y, :] = f_sweep
    g_sweep = jnp.zeros_like(f_sweep)
    for z in range(layers - 1, -1, -1):
        g_sweep = (1.0 - D[total - start - z]) * (R[z] + g_sweep)
    MSG[1, 0:span_y, :] = g_sweep

    for i in range(1, nz):
        peer = (gz + i) % nz

        @pl.when(peer > gz)
        def _():
            remote(MSG.at[0], MR.at[gz], zs.at[peer], zr.at[gz], gy, peer).start()

        @pl.when(peer < gz)
        def _():
            remote(MSG.at[1], MR.at[gz], zs.at[peer], zr.at[gz], gy, peer).start()

    MR[gz] = MSG[0]
    for i in range(1, nz):
        peer = (gz + i) % nz
        remote(MSG.at[0], MR.at[peer], zs.at[peer], zr.at[peer], gy, peer).wait_recv()

    f = jnp.zeros_like(f_sweep)
    g = jnp.zeros_like(f_sweep)
    for s in range(nz):
        f = jnp.where(s < gz, MR[s, 0:span_y, :] + PHI[s] * f, f)
    for s in range(nz - 1, -1, -1):
        g = jnp.where(s > gz, MR[s, 0:span_y, :] + PHI[nz - 1 - s] * g, g)
    line = jnp.concatenate([MR[s, span_y:, :] for s in range(nz)], 0)
    level = jnp.dot(FREE[...], line, precision=highest, preferred_element_type=jnp.float32)
    plain = LAM[...] > 0.0
    for z in range(layers):
        f = (1.0 - D[start + z + 1]) * (R[z] + f)
        R[z] = f
    d_low, d_high = D[start + layers], D[total - start - layers]
    below = d_low + d_high - d_low * d_high
    p = (f + (1.0 - d_low) * g) / jnp.where(plain, below, 1.0)
    R[layers - 1] = p
    for z in range(layers - 2, -1, -1):
        p = (1.0 - D[start + z + 1]) * p + R[z]
        R[z] = p
    flat2 = A2.reshape(ny * half_rows, 128)
    for z in range(0, layers, 2):
        pair = jnp.concatenate(
            [jnp.where(plain, R[z + k], level[z + k : z + k + 1, :]) for k in range(2)], 1
        )
        res = y_transform(pair, TY[1])
        for k in range(2):
            flat2[pl.ds(z + k, span_y, stride=layers), :] = res[:, k * 128 : (k + 1) * 128]

    def send_back(i, carry):
        peer = (gy + i) % ny
        remote(A2.at[peer], B2.at[gy], bs.at[peer], br.at[gy], peer, gz).start()
        return carry

    lax.fori_loop(1, ny, send_back, 0)
    B2[gy] = A2[gy]

    width = length // chunks
    for i in range(chunks):
        k = (gy // 2 + chunks - i) % chunks
        for side in range(2):
            peer = 2 * k + side

            @pl.when(peer != gy)
            def _():
                remote(
                    A2.at[peer], B2.at[peer], bs.at[peer], br.at[peer], peer, gz
                ).wait_recv()

        high, low = split_rows(jnp.concatenate([B2[2 * k], B2[2 * k + 1]], 1))
        both = jnp.concatenate([high, low], 0)
        span = pl.ds(pl.multiple_of(k * 256, 256), 256)
        for c in range(chunks):
            wide = dot32(both, HH[c, span, :])
            part = wide[:half_rows] + wide[half_rows:] + dot32(high, HL[c, span, :])
            part = part.reshape(rows, layers, width)
            cols = slice(c * width, (c + 1) * width)
            if i:
                part = part + PR[1 : rows + 1, :, cols]
            PR[1 : rows + 1, :, cols] = part
    pr_up = remote(PR.at[rows], PR.at[0], hs.at[6], hr.at[6], up_y, gz)
    pz_up = remote(QZS, QZR, hs.at[7], hr.at[7], gy, gz + 1)
    pr_up.start()
    for y in range(rows):
        QZS[y : y + 1, :] = PR[y + 1, layers - 1 : layers, :]

    @pl.when(has_up)
    def _():
        pz_up.start()

    @pl.when(gz == 0)
    def _():
        for y in range(rows):
            QZR[y : y + 1, :] = PR[y + 1, 0:1, :]

    @pl.when(has_down)
    def _():
        pz_up.wait_recv()

    pr_up.wait_recv()

    def project(y, carry):
        p = PR[y + 1]
        zm = jnp.where(zi == 0, QZR[pl.ds(y, 1), :], pltpu.roll(p, 1, 0))
        OM[0, y] = P0[y] - (p - pltpu.roll(p, 1, 1))
        OM[1, y] = P1[y] - (p - PR[y])
        OM[2, y] = P2[y] - (p - zm)
        return carry

    lax.fori_loop(0, rows, project, 0)

    @pl.when(has_down)
    def _():
        z_down.wait_send()
        p2_down.wait_send()

    @pl.when(has_up)
    def _():
        z_up.wait_send()
        pz_up.wait_send()

    for copy in (y_down, y_up, p1_down, pr_up):
        copy.wait_send()

    def finish(i, carry):
        peer = (gy + i) % ny
        remote(A.at[peer], B.at[gy], as_.at[peer], ar.at[gy], peer, gz).wait_send()
        remote(A2.at[peer], B2.at[gy], bs.at[peer], br.at[gy], peer, gz).wait_send()
        return carry

    lax.fori_loop(1, ny, finish, 0)
    for i in range(1, nz):
        peer = (gz + i) % nz
        remote(MSG.at[0], MR.at[gz], zs.at[peer], zr.at[gz], gy, peer).wait_send()


def fused_step(ny, nz, motion, thermal, flow, base):
    rows, layers, length = thermal.shape
    span_y, span_z = ny * rows, nz * layers
    constants = [jnp.asarray(t) for t in tables(length, span_y, span_z, ny, nz)]
    f32, b16 = jnp.float32, jnp.bfloat16
    flat = rows * layers
    vmem, dma = pltpu.VMEM, pltpu.SemaphoreType.DMA
    scratch = [
        vmem((5, rows + 2, layers, length), f32),
        vmem(flow.shape, b16),
        vmem(base.shape, b16),
        vmem(constants[0].shape, b16),
        vmem(constants[1].shape, b16),
        vmem(constants[2].shape, b16),
        vmem((span_y, 128), f32),
        vmem((layers, span_z), f32),
        vmem((2, 5, rows, length), f32),
        vmem((2, 5, rows, length), f32),
        vmem((rows, layers, length), f32),
        vmem((rows + 1, layers, length), f32),
        vmem((rows, layers, length), f32),
        vmem((rows, length), f32),
        vmem((rows, length), f32),
        vmem((2 * flat, length), b16),
        vmem((ny, flat, 128), f32),
        vmem((ny, flat, 128), f32),
        vmem((span_z + 1, span_y, 128), f32),
        vmem((nz, span_y, 128), f32),
        vmem((layers, span_y, 128), f32),
        vmem((2, span_y + layers, 128), f32),
        vmem((nz, span_y + layers, 128), f32),
        vmem((ny, flat, 128), f32),
        vmem((ny, flat, 128), f32),
        vmem((rows + 1, layers, length), f32),
        vmem((rows, length), f32),
        vmem((rows, length), f32),
        dma((9,)),
        dma((8,)),
        dma((8,)),
        dma((ny,)),
        dma((ny,)),
        dma((ny,)),
        dma((ny,)),
        dma((nz,)),
        dma((nz,)),
    ]
    hbm = pl.BlockSpec(memory_space=pltpu.HBM)
    local = pl.BlockSpec(memory_space=pltpu.VMEM)
    return pl.pallas_call(
        functools.partial(fused_kernel, ny, nz),
        out_shape=(
            jax.ShapeDtypeStruct(motion.shape, f32),
            jax.ShapeDtypeStruct(thermal.shape, f32),
        ),
        in_specs=[hbm] * 9,
        out_specs=(local, local),
        scratch_shapes=scratch,
        compiler_params=pltpu.CompilerParams(
            collective_id=0, has_side_effects=True, vmem_limit_bytes=62 * 2**20
        ),
        cost_estimate=pl.CostEstimate(
            flops=12 * flat * length * length, bytes_accessed=10 * 2**20, transcendentals=0
        ),
    )(motion, thermal, flow, base, *constants)


def solution(mesh):
    placed = (
        P(None, "gy", "gz", None),
        P("gy", "gz", None),
        P(None, "gy", "gz", None),
        P("gy", "gz", None),
    )
    groups_y, groups_z = mesh.shape["gy"], mesh.shape["gz"]

    def step(motion, thermal, flow, base):
        rows, layers, length = thermal.shape
        if length == 128 * groups_y and groups_y % 2 == 0 and rows == 8 and layers == 16:
            return fused_step(groups_y, groups_z, motion, thermal, flow, base)
        return on_device(motion, thermal, flow, base)

    return jax.shard_map(
        step,
        mesh=mesh,
        in_specs=placed,
        out_specs=(P(None, "gy", "gz", None), P("gy", "gz", None)),
        check_vma=False,
    )
```

```python
import functools
import math

import jax
import jax.numpy as jnp
import ml_dtypes
import numpy as np
from jax import lax
from jax.experimental import pallas as pl
from jax.experimental.pallas import tpu as pltpu
from jax.sharding import PartitionSpec as P

time_step = 0.2
viscosity = 0.1
diffusivity = 0.1
buoyancy = 1.0
highest = lax.Precision.HIGHEST


def padded(cells, sides, width):
    for axis, dim in sides:
        count = lax.axis_size(axis)
        head = lax.slice_in_dim(cells, 0, width, axis=dim)
        tail = lax.slice_in_dim(cells, cells.shape[dim] - width, cells.shape[dim], axis=dim)
        cells = jnp.concatenate(
            [
                lax.ppermute(tail, axis, [(i, (i + 1) % count) for i in range(count)]),
                cells,
                lax.ppermute(head, axis, [((i + 1) % count, i) for i in range(count)]),
            ],
            axis=dim,
        )
    return cells


def shifted(value, axis, by):
    length = lax.axis_size(axis)
    return lax.ppermute(value, axis, [(i, (i + by) % length) for i in range(length)])


def from_behind(block, axis, distance):
    devices = range(lax.axis_size(axis))
    route = [(i - distance, i) for i in devices if i - distance in devices]
    return lax.ppermute(block, axis, route)


def tendency_contributions(haloed_quantities, motion_pieces):
    centre = haloed_quantities[:, 1:-1, 1:-1]
    slope_x = 0.5 * (jnp.roll(centre, -1, axis=3) - jnp.roll(centre, 1, axis=3))
    slope_y = 0.5 * (haloed_quantities[:, 2:, 1:-1] - haloed_quantities[:, :-2, 1:-1])
    slope_z = 0.5 * (haloed_quantities[:, 1:-1, 2:] - haloed_quantities[:, 1:-1, :-2])
    laplace = (
        jnp.roll(centre[:4], -1, axis=3)
        + jnp.roll(centre[:4], 1, axis=3)
        + (haloed_quantities[:4, 2:, 1:-1] + haloed_quantities[:4, :-2, 1:-1])
        + (haloed_quantities[:4, 1:-1, 2:] + haloed_quantities[:4, 1:-1, :-2])
        - 6.0 * centre[:4]
    )
    advect = (
        motion_pieces[0] * slope_x[:4]
        + motion_pieces[1] * slope_y[:4]
        + motion_pieces[2] * slope_z[:4]
    )
    heat_slope = jnp.stack([slope_x[4], slope_y[4], slope_z[4]])
    unprojected_motion = centre[:3] + time_step * (
        advect[:3] + viscosity * laplace[:3] + centre[3] * heat_slope
    )
    thermal_following = centre[3] + time_step * (
        advect[3] + diffusivity * laplace[3] + buoyancy * centre[2]
    )
    return (unprojected_motion, thermal_following)


def cas_table(length):
    indices = jnp.arange(length, dtype=jnp.int32)
    phases = indices[:, None] * indices[None, :] % length
    angles = phases.astype(jnp.float32) * (2.0 * math.pi / length)
    return jnp.cos(angles) + jnp.sin(angles)


def cosine_table(length):
    indices = jnp.arange(length, dtype=jnp.int32)
    phases = indices[None, :] * (2 * indices[:, None] + 1) % (4 * length)
    return jnp.cos(phases.astype(jnp.float32) * (math.pi / (2 * length)))


def cosine_inverse(length):
    indices = jnp.arange(length, dtype=jnp.int32)
    weights = jnp.where(indices == 0, 1.0, 2.0).astype(jnp.float32)
    return cosine_table(length).T * weights[:, None] / length


def eigen_periodic(waves, length):
    return 2.0 - 2.0 * jnp.cos(waves.astype(jnp.float32) * (2.0 * math.pi / length))


def eigen_wall(waves, length):
    return 2.0 - 2.0 * jnp.cos(waves.astype(jnp.float32) * (math.pi / length))


def invert(spectral, eigen_sum):
    positive = eigen_sum > 0
    return jnp.where(positive, -spectral / jnp.where(positive, eigen_sum, 1.0), 0.0)


def wall_mask(extent, margin, position, groups):
    layer_index = jnp.arange(extent, dtype=jnp.int32)
    bottom = (layer_index < margin) & (position == 0)
    ceiling = (layer_index >= extent - margin) & (position == groups - 1)
    return jnp.where(bottom | ceiling, 0.0, 1.0).astype(jnp.float32)


def poisson(source):
    spanwise_extent, vertical_extent, lengthwise_extent = source.shape
    groups_y = lax.axis_size("gy")
    groups_z = lax.axis_size("gz")
    span_y = spanwise_extent * groups_y
    span_z = vertical_extent * groups_z
    hart_x = cas_table(lengthwise_extent)
    hart_y = cas_table(span_y)
    cos_forward = cosine_table(span_z).reshape(groups_z, vertical_extent, span_z)
    cos_backward = cosine_inverse(span_z).reshape(span_z, groups_z, vertical_extent)
    line_z = eigen_wall(jnp.arange(span_z, dtype=jnp.int32), span_z)
    piece_x = lengthwise_extent // groups_y
    quarter = span_y // groups_z
    table_x = hart_x.reshape(lengthwise_extent, groups_y, piece_x)
    table_y = hart_y.reshape(groups_y, spanwise_extent, groups_z, quarter)
    step_one = jnp.einsum("yzx,xgj->gjyz", source, table_x, precision=highest).reshape(groups_y, -1)
    step_one = lax.all_to_all(step_one, "gy", split_axis=0, concat_axis=0, tiled=True).reshape(
        groups_y, piece_x, spanwise_extent, vertical_extent
    )
    step_two = jnp.einsum("sjyz,syhq->hjqz", step_one, table_y, precision=highest).reshape(
        groups_z, -1
    )
    step_two = lax.all_to_all(step_two, "gz", split_axis=0, concat_axis=0, tiled=True).reshape(
        groups_z, piece_x, quarter, vertical_extent
    )
    spectral = jnp.einsum("tjqc,tck->jqk", step_two, cos_forward, precision=highest)
    wave_x = lax.axis_index("gy") * piece_x + jnp.arange(piece_x, dtype=jnp.int32)
    wave_y = lax.axis_index("gz") * quarter + jnp.arange(quarter, dtype=jnp.int32)
    eigen_sum = (
        eigen_periodic(wave_x, lengthwise_extent)[:, None, None]
        + eigen_periodic(wave_y, span_y)[None, :, None]
        + line_z[None, None, :]
    )
    solved = invert(spectral, eigen_sum)
    step_three = jnp.einsum("jqk,ktc->tjqc", solved, cos_backward, precision=highest).reshape(
        groups_z, -1
    )
    step_three = lax.all_to_all(step_three, "gz", split_axis=0, concat_axis=0, tiled=True).reshape(
        groups_z, piece_x, quarter, vertical_extent
    )
    step_four = (
        jnp.einsum("hjqz,syhq->sjyz", step_three, table_y, precision=highest) * (1.0 / span_y)
    ).reshape(groups_y, -1)
    step_four = lax.all_to_all(step_four, "gy", split_axis=0, concat_axis=0, tiled=True).reshape(
        groups_y, piece_x, spanwise_extent, vertical_extent
    )
    return jnp.einsum("gjyz,xgj->yzx", step_four, table_x, precision=highest) * (
        1.0 / lengthwise_extent
    )


def on_device(dual_flow_speeds, dual_thermal_state, forward_flow_speeds, forward_thermal_state):
    spanwise_extent, vertical_extent, lengthwise_extent = dual_thermal_state.shape
    groups_z = lax.axis_size("gz")
    place_z = lax.axis_index("gz")
    motion_pieces = forward_flow_speeds.astype(jnp.float32)
    forward_thermal_flux = forward_thermal_state.astype(jnp.float32)
    stacked_fields = jnp.concatenate(
        [dual_flow_speeds, dual_thermal_state[None], forward_thermal_flux[None]], 0
    )
    haloed_quantities = padded(stacked_fields, (("gy", 1), ("gz", 2)), 1)
    haloed_quantities = (
        haloed_quantities
        * wall_mask(vertical_extent + 2, 1, place_z, groups_z)[None, None, :, None]
    )
    unprojected_motion, advanced_dual_thermal = tendency_contributions(
        haloed_quantities, motion_pieces
    )
    upper_y = shifted(unprojected_motion[1][0], "gy", -1)
    upper_z = from_behind(unprojected_motion[2][:, 0], "gz", -1)
    next_y = jnp.concatenate([unprojected_motion[1][1:], upper_y[None]], 0)
    next_z = jnp.concatenate([unprojected_motion[2][:, 1:], upper_z[:, None]], 1)
    source = (
        jnp.roll(unprojected_motion[0], -1, axis=2)
        - unprojected_motion[0]
        + (next_y - unprojected_motion[1])
        + (next_z - unprojected_motion[2])
    )
    pressure = poisson(source)
    grad_x = pressure - jnp.roll(pressure, 1, axis=2)
    lower_y = shifted(pressure[spanwise_extent - 1], "gy", 1)
    grad_y = pressure - jnp.concatenate([lower_y[None], pressure[:-1]], 0)
    lower_z = from_behind(pressure[:, vertical_extent - 1], "gz", 1)
    below = jnp.concatenate([lower_z[:, None], pressure[:, :-1]], 1)
    floor_layer = (jnp.arange(vertical_extent, dtype=jnp.int32) == 0) & (place_z == 0)
    grad_z = jnp.where(floor_layer[None, :, None], 0.0, pressure - below)
    advanced_dual_motion = unprojected_motion - jnp.stack([grad_x, grad_y, grad_z])
    return (advanced_dual_motion, advanced_dual_thermal)


def halves(table):
    high = table.astype(np.float32).astype(ml_dtypes.bfloat16)
    low = (table - high.astype(np.float64)).astype(np.float32).astype(ml_dtypes.bfloat16)
    return high, low


def cas_np(length):
    phases = np.outer(np.arange(length), np.arange(length)) % length
    angles = phases * (2.0 * np.pi / length)
    return np.cos(angles) + np.sin(angles)


@functools.lru_cache(maxsize=None)
def tables(length, span_y, span_z, groups_y, groups_z):
    hart_x = cas_np(length)
    chunks = groups_y // 2
    hx = [
        np.ascontiguousarray(t.reshape(length, chunks, length // chunks).transpose(1, 0, 2))
        for t in halves(hart_x)
    ]
    hart_y = cas_np(span_y)
    forward = halves(hart_y * (-1.0 / (span_y * length)))
    backward = halves(hart_y)
    ty = np.stack([np.concatenate([hi, hi, lo], 1) for hi, lo in (forward, backward)])
    line_x = 4.0 * np.sin(np.pi * np.arange(length) / length) ** 2
    line_y = 4.0 * np.sin(np.pi * np.arange(span_y) / span_y) ** 2
    modes = (line_x[None, :] + line_y[:, None]).astype(np.float32)
    modes = np.ascontiguousarray(modes.reshape(span_y, groups_y, -1).transpose(1, 0, 2))
    k = np.arange(span_z)
    basis = np.cos(np.pi * np.outer(k, 2 * k + 1) / (2 * span_z))
    eig = 4.0 * np.sin(np.pi * k / (2 * span_z)) ** 2
    scale = np.where(k == 0, 0.0, 2.0 / (span_z * np.where(k == 0, 1.0, eig)))
    mean_free = (basis.T * scale) @ basis
    mean_free = mean_free.astype(np.float32).reshape(groups_z, -1, span_z)
    return hx[0], hx[1], ty, modes, mean_free


def split_rows(value):
    high = value.astype(jnp.bfloat16)
    return high, (value - high.astype(jnp.float32)).astype(jnp.bfloat16)


def dot32(a, b):
    return jnp.dot(a, b, preferred_element_type=jnp.float32)


def fused_kernel(
    ny, nz, motion, thermal, flow, base, hx_hi, hx_lo, ty_in, modes_in, free_in,
    out_p, out_t, out_pr, out_z,
    F, U, TH, HH, HL, TY, LAM, FREE, ZS, ZR, P0, P1, P2, PZS, PZR, S, A, B, D, PHI,
    R, MSG, MR, A2, B2, PR, QZS, QZR, OT, ZT, UZ, lsem, osem, ps, pr_, qs, qr, hs, hr, as_, ar, bs, br, zs, zr,
):
    gy, gz = lax.axis_index("gy"), lax.axis_index("gz")
    rows, layers, length = thermal.shape
    mesh_id = pl.DeviceIdType.MESH
    up_y, down_y = (gy + 1) % ny, (gy + ny - 1) % ny
    has_up, has_down = gz < nz - 1, gz > 0

    loads = [
        pltpu.make_async_copy(motion, F.at[0:3, 1 : rows + 1], lsem.at[0]),
        pltpu.make_async_copy(thermal, F.at[3, 1 : rows + 1], lsem.at[1]),
        pltpu.make_async_copy(base, TH, lsem.at[2]),
        pltpu.make_async_copy(flow, U, lsem.at[3]),
        pltpu.make_async_copy(modes_in.at[gy], LAM, lsem.at[4]),
        pltpu.make_async_copy(free_in.at[gz], FREE, lsem.at[5]),
        pltpu.make_async_copy(ty_in, TY, lsem.at[6]),
        pltpu.make_async_copy(hx_hi, HH, lsem.at[7]),
        pltpu.make_async_copy(hx_lo, HL, lsem.at[8]),
    ]
    for copy in loads:
        copy.start()

    barrier = pltpu.get_barrier_semaphore()
    for i in range(1, ny):
        pl.semaphore_signal(
            barrier, inc=1, device_id=((gy + i) % ny, gz), device_id_type=mesh_id
        )
    for i in range(1, nz):
        pl.semaphore_signal(
            barrier, inc=1, device_id=(gy, (gz + i) % nz), device_id_type=mesh_id
        )

    def remote(src, dst, ssem, rsem, y, z):
        return pltpu.make_async_remote_copy(
            src_ref=src, dst_ref=dst, send_sem=ssem, recv_sem=rsem,
            device_id=(y, z), device_id_type=mesh_id,
        )

    loads[2].wait()
    for y in range(rows):
        F[4, y + 1] = TH[y].astype(jnp.float32)
    loads[0].wait()
    loads[1].wait()
    for f in range(5):
        for y in range(rows):
            ZS[0, f, y : y + 1, :] = F[f, y + 1, 0:1, :]
            ZS[1, f, y : y + 1, :] = F[f, y + 1, layers - 1 : layers, :]
    pl.semaphore_wait(barrier, ny + nz - 2)

    z_down = remote(ZS.at[0], ZR.at[1], hs.at[0], hr.at[0], gy, gz - 1)
    z_up = remote(ZS.at[1], ZR.at[0], hs.at[1], hr.at[1], gy, gz + 1)
    y_down = remote(F.at[:, 1], F.at[:, rows + 1], hs.at[2], hr.at[2], down_y, gz)
    y_up = remote(F.at[:, rows], F.at[:, 0], hs.at[3], hr.at[3], up_y, gz)

    @pl.when(has_down)
    def _():
        z_down.start()

    @pl.when(has_up)
    def _():
        z_up.start()

    y_down.start()
    y_up.start()

    @pl.when(gz == 0)
    def _():
        ZR[0] = jnp.zeros_like(ZR[0])

    @pl.when(gz == nz - 1)
    def _():
        ZR[1] = jnp.zeros_like(ZR[1])
        PZR[...] = jnp.zeros_like(PZR)

    loads[4].wait()
    D[0] = jnp.zeros_like(D[0])

    def ratios(block, carry):
        def one(i, prod):
            at = block * layers + i
            e = LAM[...] + D[at]
            d = e / (1.0 + e)
            D[at + 1] = d
            return prod * (1.0 - d)

        PHI[block] = lax.fori_loop(0, layers, one, jnp.ones_like(LAM[...]))
        return carry

    lax.fori_loop(0, nz, ratios, 0)

    loads[3].wait()
    for y in range(rows):
        for i, f in enumerate((2, 4)):
            ZT[i, y : y + 1, :] = F[f, y + 1, 1:2, :]
        for d in range(3):
            UZ[d, y : y + 1, :] = U[d, y].astype(jnp.float32)[0:1, :]

    @pl.when(has_up)
    def _():
        z_down.wait_recv()

    @pl.when(has_down)
    def _():
        z_up.wait_recv()

    zi = lax.broadcasted_iota(jnp.int32, (layers, length), 0)

    def stencil(y, carry):
        def sides(f):
            c = F[f, y + 1]
            xp, xm = pltpu.roll(c, length - 1, 1), pltpu.roll(c, 1, 1)
            zp = jnp.where(zi == layers - 1, ZR[1, f, pl.ds(y, 1), :], pltpu.roll(c, layers - 1, 0))
            zm = jnp.where(zi == 0, ZR[0, f, pl.ds(y, 1), :], pltpu.roll(c, 1, 0))
            return c, xp, xm, F[f, y + 2], F[f, y], zp, zm

        u0, u1, u2 = (U[d, y].astype(jnp.float32) for d in range(3))

        def advance(f):
            c, xp, xm, yp, ym, zp, zm = sides(f)
            adv = 0.5 * (u0 * (xp - xm) + u1 * (yp - ym) + u2 * (zp - zm))
            lap = (xp + xm) + (yp + ym) + (zp + zm) - 6.0 * c
            return c, adv + viscosity * lap

        c3, t3 = advance(3)
        _, hxp, hxm, hyp, hym, hzp, hzm = sides(4)
        half = 0.5 * c3
        c, t = advance(0)
        P0[y] = c + time_step * (t + half * (hxp - hxm))
        c, t = advance(1)
        P1[y] = c + time_step * (t + half * (hyp - hym))
        c, t = advance(2)
        p2 = c + time_step * (t + half * (hzp - hzm))
        P2[y] = p2
        OT[y] = c3 + time_step * (t3 + buoyancy * c)
        return carry

    p1_down = remote(P1.at[0], P1.at[rows], hs.at[4], hr.at[4], down_y, gz)
    p2_down = remote(PZS, PZR, hs.at[5], hr.at[5], gy, gz - 1)
    inner = rows // 2
    lax.fori_loop(1, inner, stencil, 0)
    y_down.wait_recv()
    y_up.wait_recv()
    stencil(0, 0)
    p1_down.start()

    yi = lax.broadcasted_iota(jnp.int32, (rows, length), 0)
    c = ZS[0, 2]
    xp, xm = pltpu.roll(c, length - 1, 1), pltpu.roll(c, 1, 1)
    yp = jnp.where(yi == rows - 1, F[2, rows + 1, 0:1, :], pltpu.roll(c, rows - 1, 0))
    ym = jnp.where(yi == 0, F[2, 0, 0:1, :], pltpu.roll(c, 1, 0))
    zp, zm = ZT[0], ZR[0, 2]
    adv = 0.5 * (UZ[0] * (xp - xm) + UZ[1] * (yp - ym) + UZ[2] * (zp - zm))
    lap = (xp + xm) + (yp + ym) + (zp + zm) - 6.0 * c
    PZS[...] = c + time_step * (
        adv + viscosity * lap + 0.5 * ZS[0, 3] * (ZT[1] - ZR[0, 4])
    )

    @pl.when(has_down)
    def _():
        p2_down.start()

    lax.fori_loop(inner, rows, stencil, 0)
    outs = [
        pltpu.make_async_copy(OT, out_t, osem.at[0]),
        pltpu.make_async_copy(P0, out_p.at[0], osem.at[1]),
        pltpu.make_async_copy(P1.at[0:rows], out_p.at[1], osem.at[2]),
        pltpu.make_async_copy(P2, out_p.at[2], osem.at[3]),
    ]
    for copy in outs:
        copy.start()

    @pl.when(has_up)
    def _():
        p2_down.wait_recv()

    p1_down.wait_recv()
    half_rows = rows * layers

    def diverge(y, carry):
        p0, p2 = P0[y], P2[y]
        zp = jnp.where(zi == layers - 1, PZR[pl.ds(y, 1), :], pltpu.roll(p2, layers - 1, 0))
        s = (pltpu.roll(p0, length - 1, 1) - p0) + (P1[y + 1] - P1[y]) + (zp - p2)
        high, low = split_rows(s)
        S[pl.ds(pl.multiple_of(y * layers, layers), layers), :] = high
        S[pl.ds(pl.multiple_of(half_rows + y * layers, layers), layers), :] = low
        return carry

    lax.fori_loop(0, rows, diverge, 0)

    loads[7].wait()
    loads[8].wait()
    chunks = ny // 2

    def x_forward(i, carry):
        c = (gy // 2 + 1 + i) % chunks
        wide = dot32(S[...], HH[c])
        part = wide[:half_rows] + wide[half_rows:] + dot32(S[0:half_rows, :], HL[c])
        for side in range(2):
            peer = 2 * c + side
            A[peer] = part[:, side * 128 : (side + 1) * 128]

            @pl.when(peer != gy)
            def _():
                remote(A.at[peer], B.at[gy], as_.at[peer], ar.at[gy], peer, gz).start()

            @pl.when(peer == gy)
            def _():
                B[peer] = A[peer]

        return carry

    lax.fori_loop(0, chunks, x_forward, 0)
    loads[5].wait()
    loads[6].wait()

    def wait_all(src, dst, ssem, rsem):
        def one(i, carry):
            peer = (gy + i) % ny
            remote(src.at[peer], dst.at[peer], ssem.at[peer], rsem.at[peer], peer, gz).wait_recv()
            return carry

        lax.fori_loop(1, ny, one, 0)

    wait_all(A, B, as_, ar)
    span_y = ny * rows
    flat = B.reshape(ny * half_rows, 128)

    def y_transform(pair, table):
        high, low = split_rows(pair)
        return dot32(table, jnp.concatenate([high, low, high], 0))

    f_sweep = None
    start = gz * layers
    total = nz * layers
    for z in range(0, layers, 2):
        pair = jnp.concatenate(
            [flat[pl.ds(z + k, span_y, stride=layers), :] for k in range(2)], 1
        )
        res = y_transform(pair, TY[0])
        for k in range(2):
            r = res[:, k * 128 : (k + 1) * 128]
            R[z + k] = r
            MSG[0, span_y + z + k : span_y + z + k + 1, :] = r[0:1, :]
            MSG[1, span_y + z + k : span_y + z + k + 1, :] = r[0:1, :]
            w = 1.0 - D[start + z + k + 1]
            f_sweep = w * (r if f_sweep is None else r + f_sweep)
    MSG[0, 0:span_y, :] = f_sweep
    g_sweep = jnp.zeros_like(f_sweep)
    for z in range(layers - 1, -1, -1):
        g_sweep = (1.0 - D[total - start - z]) * (R[z] + g_sweep)
    MSG[1, 0:span_y, :] = g_sweep

    for i in range(1, nz):
        peer = (gz + i) % nz

        @pl.when(peer > gz)
        def _():
            remote(MSG.at[0], MR.at[gz], zs.at[peer], zr.at[gz], gy, peer).start()

        @pl.when(peer < gz)
        def _():
            remote(MSG.at[1], MR.at[gz], zs.at[peer], zr.at[gz], gy, peer).start()

    MR[gz] = MSG[0]
    for i in range(1, nz):
        peer = (gz + i) % nz
        remote(MSG.at[0], MR.at[peer], zs.at[peer], zr.at[peer], gy, peer).wait_recv()

    f = jnp.zeros_like(f_sweep)
    g = jnp.zeros_like(f_sweep)
    for s in range(nz):
        f = jnp.where(s < gz, MR[s, 0:span_y, :] + PHI[s] * f, f)
    for s in range(nz - 1, -1, -1):
        g = jnp.where(s > gz, MR[s, 0:span_y, :] + PHI[nz - 1 - s] * g, g)
    line = jnp.concatenate([MR[s, span_y:, :] for s in range(nz)], 0)
    level = jnp.dot(FREE[...], line, precision=highest, preferred_element_type=jnp.float32)
    plain = LAM[...] > 0.0
    for z in range(layers):
        f = (1.0 - D[start + z + 1]) * (R[z] + f)
        R[z] = f
    d_low, d_high = D[start + layers], D[total - start - layers]
    below = d_low + d_high - d_low * d_high
    p = (f + (1.0 - d_low) * g) / jnp.where(plain, below, 1.0)
    R[layers - 1] = p
    for z in range(layers - 2, -1, -1):
        p = (1.0 - D[start + z + 1]) * p + R[z]
        R[z] = p
    flat2 = A2.reshape(ny * half_rows, 128)
    for z in range(0, layers, 2):
        pair = jnp.concatenate(
            [jnp.where(plain, R[z + k], level[z + k : z + k + 1, :]) for k in range(2)], 1
        )
        res = y_transform(pair, TY[1])
        for k in range(2):
            flat2[pl.ds(z + k, span_y, stride=layers), :] = res[:, k * 128 : (k + 1) * 128]

    def send_back(i, carry):
        peer = (gy + i) % ny
        remote(A2.at[peer], B2.at[gy], bs.at[peer], br.at[gy], peer, gz).start()
        return carry

    lax.fori_loop(1, ny, send_back, 0)
    B2[gy] = A2[gy]

    width = length // chunks

    def edge(c):
        cols = slice(c * width, (c + 1) * width)
        return (
            remote(
                PR.at[rows, :, cols], PR.at[0, :, cols], ps.at[c], pr_.at[c], up_y, gz
            ),
            remote(QZS.at[:, cols], QZR.at[:, cols], qs.at[c], qr.at[c], gy, gz + 1),
        )

    for i in range(chunks):
        k = (gy // 2 + chunks - i) % chunks
        for side in range(2):
            peer = 2 * k + side

            @pl.when(peer != gy)
            def _():
                remote(
                    A2.at[peer], B2.at[peer], bs.at[peer], br.at[peer], peer, gz
                ).wait_recv()

        high, low = split_rows(jnp.concatenate([B2[2 * k], B2[2 * k + 1]], 1))
        both = jnp.concatenate([high, low], 0)
        span = pl.ds(pl.multiple_of(k * 256, 256), 256)
        for c in range(chunks):
            wide = dot32(both, HH[c, span, :])
            part = wide[:half_rows] + wide[half_rows:] + dot32(high, HL[c, span, :])
            part = part.reshape(rows, layers, width)
            cols = slice(c * width, (c + 1) * width)
            if i:
                part = part + PR[1 : rows + 1, :, cols]
            PR[1 : rows + 1, :, cols] = part
            if i == chunks - 1:
                QZS[:, cols] = jnp.concatenate(
                    [part[y, layers - 1 : layers, :] for y in range(rows)], 0
                )
                pr_up, pz_up = edge(c)
                pr_up.start()

                @pl.when(has_up)
                def _():
                    pz_up.start()

    @pl.when(gz == 0)
    def _():
        for y in range(rows):
            QZR[y : y + 1, :] = PR[y + 1, 0:1, :]

    for c in range(chunks):
        pr_up, pz_up = edge(c)
        pr_up.wait_recv()

        @pl.when(has_down)
        def _():
            pz_up.wait_recv()

    last = [
        pltpu.make_async_copy(PR, out_pr, osem.at[4]),
        pltpu.make_async_copy(QZR, out_z, osem.at[5]),
    ]
    for copy in last:
        copy.start()

    @pl.when(has_down)
    def _():
        z_down.wait_send()
        p2_down.wait_send()

    @pl.when(has_up)
    def _():
        z_up.wait_send()
        for c in range(chunks):
            edge(c)[1].wait_send()

    for c in range(chunks):
        edge(c)[0].wait_send()
    for copy in (y_down, y_up, p1_down):
        copy.wait_send()

    def finish(i, carry):
        peer = (gy + i) % ny
        remote(A.at[peer], B.at[gy], as_.at[peer], ar.at[gy], peer, gz).wait_send()
        remote(A2.at[peer], B2.at[gy], bs.at[peer], br.at[gy], peer, gz).wait_send()
        return carry

    lax.fori_loop(1, ny, finish, 0)
    for i in range(1, nz):
        peer = (gz + i) % nz
        remote(MSG.at[0], MR.at[gz], zs.at[peer], zr.at[gz], gy, peer).wait_send()
    for copy in outs + last:
        copy.wait()


def project_kernel(prov, pressure, lower, thermal, out_motion, out_thermal):
    _, count, layers, length = prov.shape
    first = pl.program_id(0) * count
    zi = lax.broadcasted_iota(jnp.int32, (layers, length), 0)
    for y in range(count):
        p = pressure[first + y + 1]
        zm = jnp.where(zi == 0, lower[pl.ds(first + y, 1), :], pltpu.roll(p, 1, 0))
        out_motion[0, y] = prov[0, y] - (p - pltpu.roll(p, 1, 1))
        out_motion[1, y] = prov[1, y] - (p - pressure[first + y])
        out_motion[2, y] = prov[2, y] - (p - zm)
    out_thermal[...] = thermal[...]


def fused_step(ny, nz, motion, thermal, flow, base):
    rows, layers, length = thermal.shape
    span_y, span_z = ny * rows, nz * layers
    constants = [jnp.asarray(t) for t in tables(length, span_y, span_z, ny, nz)]
    f32, b16 = jnp.float32, jnp.bfloat16
    flat = rows * layers
    vmem, dma = pltpu.VMEM, pltpu.SemaphoreType.DMA
    scratch = [
        vmem((5, rows + 2, layers, length), f32),
        vmem(flow.shape, b16),
        vmem(base.shape, b16),
        vmem(constants[0].shape, b16),
        vmem(constants[1].shape, b16),
        vmem(constants[2].shape, b16),
        vmem((span_y, 128), f32),
        vmem((layers, span_z), f32),
        vmem((2, 5, rows, length), f32),
        vmem((2, 5, rows, length), f32),
        vmem((rows, layers, length), f32),
        vmem((rows + 1, layers, length), f32),
        vmem((rows, layers, length), f32),
        vmem((rows, length), f32),
        vmem((rows, length), f32),
        vmem((2 * flat, length), b16),
        vmem((ny, flat, 128), f32),
        vmem((ny, flat, 128), f32),
        vmem((span_z + 1, span_y, 128), f32),
        vmem((nz, span_y, 128), f32),
        vmem((layers, span_y, 128), f32),
        vmem((2, span_y + layers, 128), f32),
        vmem((nz, span_y + layers, 128), f32),
        vmem((ny, flat, 128), f32),
        vmem((ny, flat, 128), f32),
        vmem((rows + 1, layers, length), f32),
        vmem((rows, length), f32),
        vmem((rows, length), f32),
        vmem((rows, layers, length), f32),
        vmem((2, rows, length), f32),
        vmem((3, rows, length), f32),
        dma((9,)),
        dma((6,)),
        dma((ny // 2,)),
        dma((ny // 2,)),
        dma((ny // 2,)),
        dma((ny // 2,)),
        dma((6,)),
        dma((6,)),
        dma((ny,)),
        dma((ny,)),
        dma((ny,)),
        dma((ny,)),
        dma((nz,)),
        dma((nz,)),
    ]
    hbm = pl.BlockSpec(memory_space=pltpu.HBM)
    prov, advanced, pressure, lower = pl.pallas_call(
        functools.partial(fused_kernel, ny, nz),
        out_shape=(
            jax.ShapeDtypeStruct(motion.shape, f32),
            jax.ShapeDtypeStruct(thermal.shape, f32),
            jax.ShapeDtypeStruct((rows + 1, layers, length), f32),
            jax.ShapeDtypeStruct((rows, length), f32),
        ),
        in_specs=[hbm] * 9,
        out_specs=(hbm,) * 4,
        scratch_shapes=scratch,
        compiler_params=pltpu.CompilerParams(
            collective_id=0, has_side_effects=True, vmem_limit_bytes=62 * 2**20
        ),
        cost_estimate=pl.CostEstimate(
            flops=12 * flat * length * length, bytes_accessed=10 * 2**20, transcendentals=0
        ),
    )(motion, thermal, flow, base, *constants)
    count = rows // 4
    fields = pl.BlockSpec((3, count, layers, length), lambda i: (0, i, 0, 0))
    single = pl.BlockSpec((count, layers, length), lambda i: (i, 0, 0))
    return pl.pallas_call(
        project_kernel,
        grid=(4,),
        out_shape=(
            jax.ShapeDtypeStruct(motion.shape, f32),
            jax.ShapeDtypeStruct(thermal.shape, f32),
        ),
        in_specs=[
            fields,
            pl.BlockSpec((rows + 1, layers, length), lambda i: (0, 0, 0)),
            pl.BlockSpec((rows, length), lambda i: (0, 0)),
            single,
        ],
        out_specs=(fields, single),
        compiler_params=pltpu.CompilerParams(vmem_limit_bytes=62 * 2**20),
    )(prov, pressure, lower, advanced)


def solution(mesh):
    placed = (
        P(None, "gy", "gz", None),
        P("gy", "gz", None),
        P(None, "gy", "gz", None),
        P("gy", "gz", None),
    )
    groups_y, groups_z = mesh.shape["gy"], mesh.shape["gz"]

    def step(motion, thermal, flow, base):
        rows, layers, length = thermal.shape
        if length == 128 * groups_y and groups_y % 2 == 0 and rows == 8 and layers == 16:
            return fused_step(groups_y, groups_z, motion, thermal, flow, base)
        return on_device(motion, thermal, flow, base)

    return jax.shard_map(
        step,
        mesh=mesh,
        in_specs=placed,
        out_specs=(P(None, "gy", "gz", None), P("gy", "gz", None)),
        check_vma=False,
    )
```

```python
import functools
import math

import jax
import jax.numpy as jnp
import ml_dtypes
import numpy as np
from jax import lax
from jax.experimental import pallas as pl
from jax.experimental.pallas import tpu as pltpu
from jax.sharding import PartitionSpec as P

time_step = 0.2
viscosity = 0.1
diffusivity = 0.1
buoyancy = 1.0
highest = lax.Precision.HIGHEST


def padded(cells, sides, width):
    for axis, dim in sides:
        count = lax.axis_size(axis)
        head = lax.slice_in_dim(cells, 0, width, axis=dim)
        tail = lax.slice_in_dim(cells, cells.shape[dim] - width, cells.shape[dim], axis=dim)
        cells = jnp.concatenate(
            [
                lax.ppermute(tail, axis, [(i, (i + 1) % count) for i in range(count)]),
                cells,
                lax.ppermute(head, axis, [((i + 1) % count, i) for i in range(count)]),
            ],
            axis=dim,
        )
    return cells


def shifted(value, axis, by):
    length = lax.axis_size(axis)
    return lax.ppermute(value, axis, [(i, (i + by) % length) for i in range(length)])


def from_behind(block, axis, distance):
    devices = range(lax.axis_size(axis))
    route = [(i - distance, i) for i in devices if i - distance in devices]
    return lax.ppermute(block, axis, route)


def tendency_contributions(haloed_quantities, motion_pieces):
    centre = haloed_quantities[:, 1:-1, 1:-1]
    slope_x = 0.5 * (jnp.roll(centre, -1, axis=3) - jnp.roll(centre, 1, axis=3))
    slope_y = 0.5 * (haloed_quantities[:, 2:, 1:-1] - haloed_quantities[:, :-2, 1:-1])
    slope_z = 0.5 * (haloed_quantities[:, 1:-1, 2:] - haloed_quantities[:, 1:-1, :-2])
    laplace = (
        jnp.roll(centre[:4], -1, axis=3)
        + jnp.roll(centre[:4], 1, axis=3)
        + (haloed_quantities[:4, 2:, 1:-1] + haloed_quantities[:4, :-2, 1:-1])
        + (haloed_quantities[:4, 1:-1, 2:] + haloed_quantities[:4, 1:-1, :-2])
        - 6.0 * centre[:4]
    )
    advect = (
        motion_pieces[0] * slope_x[:4]
        + motion_pieces[1] * slope_y[:4]
        + motion_pieces[2] * slope_z[:4]
    )
    heat_slope = jnp.stack([slope_x[4], slope_y[4], slope_z[4]])
    unprojected_motion = centre[:3] + time_step * (
        advect[:3] + viscosity * laplace[:3] + centre[3] * heat_slope
    )
    thermal_following = centre[3] + time_step * (
        advect[3] + diffusivity * laplace[3] + buoyancy * centre[2]
    )
    return (unprojected_motion, thermal_following)


def cas_table(length):
    indices = jnp.arange(length, dtype=jnp.int32)
    phases = indices[:, None] * indices[None, :] % length
    angles = phases.astype(jnp.float32) * (2.0 * math.pi / length)
    return jnp.cos(angles) + jnp.sin(angles)


def cosine_table(length):
    indices = jnp.arange(length, dtype=jnp.int32)
    phases = indices[None, :] * (2 * indices[:, None] + 1) % (4 * length)
    return jnp.cos(phases.astype(jnp.float32) * (math.pi / (2 * length)))


def cosine_inverse(length):
    indices = jnp.arange(length, dtype=jnp.int32)
    weights = jnp.where(indices == 0, 1.0, 2.0).astype(jnp.float32)
    return cosine_table(length).T * weights[:, None] / length


def eigen_periodic(waves, length):
    return 2.0 - 2.0 * jnp.cos(waves.astype(jnp.float32) * (2.0 * math.pi / length))


def eigen_wall(waves, length):
    return 2.0 - 2.0 * jnp.cos(waves.astype(jnp.float32) * (math.pi / length))


def invert(spectral, eigen_sum):
    positive = eigen_sum > 0
    return jnp.where(positive, -spectral / jnp.where(positive, eigen_sum, 1.0), 0.0)


def wall_mask(extent, margin, position, groups):
    layer_index = jnp.arange(extent, dtype=jnp.int32)
    bottom = (layer_index < margin) & (position == 0)
    ceiling = (layer_index >= extent - margin) & (position == groups - 1)
    return jnp.where(bottom | ceiling, 0.0, 1.0).astype(jnp.float32)


def poisson(source):
    spanwise_extent, vertical_extent, lengthwise_extent = source.shape
    groups_y = lax.axis_size("gy")
    groups_z = lax.axis_size("gz")
    span_y = spanwise_extent * groups_y
    span_z = vertical_extent * groups_z
    hart_x = cas_table(lengthwise_extent)
    hart_y = cas_table(span_y)
    cos_forward = cosine_table(span_z).reshape(groups_z, vertical_extent, span_z)
    cos_backward = cosine_inverse(span_z).reshape(span_z, groups_z, vertical_extent)
    line_z = eigen_wall(jnp.arange(span_z, dtype=jnp.int32), span_z)
    piece_x = lengthwise_extent // groups_y
    quarter = span_y // groups_z
    table_x = hart_x.reshape(lengthwise_extent, groups_y, piece_x)
    table_y = hart_y.reshape(groups_y, spanwise_extent, groups_z, quarter)
    step_one = jnp.einsum("yzx,xgj->gjyz", source, table_x, precision=highest).reshape(groups_y, -1)
    step_one = lax.all_to_all(step_one, "gy", split_axis=0, concat_axis=0, tiled=True).reshape(
        groups_y, piece_x, spanwise_extent, vertical_extent
    )
    step_two = jnp.einsum("sjyz,syhq->hjqz", step_one, table_y, precision=highest).reshape(
        groups_z, -1
    )
    step_two = lax.all_to_all(step_two, "gz", split_axis=0, concat_axis=0, tiled=True).reshape(
        groups_z, piece_x, quarter, vertical_extent
    )
    spectral = jnp.einsum("tjqc,tck->jqk", step_two, cos_forward, precision=highest)
    wave_x = lax.axis_index("gy") * piece_x + jnp.arange(piece_x, dtype=jnp.int32)
    wave_y = lax.axis_index("gz") * quarter + jnp.arange(quarter, dtype=jnp.int32)
    eigen_sum = (
        eigen_periodic(wave_x, lengthwise_extent)[:, None, None]
        + eigen_periodic(wave_y, span_y)[None, :, None]
        + line_z[None, None, :]
    )
    solved = invert(spectral, eigen_sum)
    step_three = jnp.einsum("jqk,ktc->tjqc", solved, cos_backward, precision=highest).reshape(
        groups_z, -1
    )
    step_three = lax.all_to_all(step_three, "gz", split_axis=0, concat_axis=0, tiled=True).reshape(
        groups_z, piece_x, quarter, vertical_extent
    )
    step_four = (
        jnp.einsum("hjqz,syhq->sjyz", step_three, table_y, precision=highest) * (1.0 / span_y)
    ).reshape(groups_y, -1)
    step_four = lax.all_to_all(step_four, "gy", split_axis=0, concat_axis=0, tiled=True).reshape(
        groups_y, piece_x, spanwise_extent, vertical_extent
    )
    return jnp.einsum("gjyz,xgj->yzx", step_four, table_x, precision=highest) * (
        1.0 / lengthwise_extent
    )


def on_device(dual_flow_speeds, dual_thermal_state, forward_flow_speeds, forward_thermal_state):
    spanwise_extent, vertical_extent, lengthwise_extent = dual_thermal_state.shape
    groups_z = lax.axis_size("gz")
    place_z = lax.axis_index("gz")
    motion_pieces = forward_flow_speeds.astype(jnp.float32)
    forward_thermal_flux = forward_thermal_state.astype(jnp.float32)
    stacked_fields = jnp.concatenate(
        [dual_flow_speeds, dual_thermal_state[None], forward_thermal_flux[None]], 0
    )
    haloed_quantities = padded(stacked_fields, (("gy", 1), ("gz", 2)), 1)
    haloed_quantities = (
        haloed_quantities
        * wall_mask(vertical_extent + 2, 1, place_z, groups_z)[None, None, :, None]
    )
    unprojected_motion, advanced_dual_thermal = tendency_contributions(
        haloed_quantities, motion_pieces
    )
    upper_y = shifted(unprojected_motion[1][0], "gy", -1)
    upper_z = from_behind(unprojected_motion[2][:, 0], "gz", -1)
    next_y = jnp.concatenate([unprojected_motion[1][1:], upper_y[None]], 0)
    next_z = jnp.concatenate([unprojected_motion[2][:, 1:], upper_z[:, None]], 1)
    source = (
        jnp.roll(unprojected_motion[0], -1, axis=2)
        - unprojected_motion[0]
        + (next_y - unprojected_motion[1])
        + (next_z - unprojected_motion[2])
    )
    pressure = poisson(source)
    grad_x = pressure - jnp.roll(pressure, 1, axis=2)
    lower_y = shifted(pressure[spanwise_extent - 1], "gy", 1)
    grad_y = pressure - jnp.concatenate([lower_y[None], pressure[:-1]], 0)
    lower_z = from_behind(pressure[:, vertical_extent - 1], "gz", 1)
    below = jnp.concatenate([lower_z[:, None], pressure[:, :-1]], 1)
    floor_layer = (jnp.arange(vertical_extent, dtype=jnp.int32) == 0) & (place_z == 0)
    grad_z = jnp.where(floor_layer[None, :, None], 0.0, pressure - below)
    advanced_dual_motion = unprojected_motion - jnp.stack([grad_x, grad_y, grad_z])
    return (advanced_dual_motion, advanced_dual_thermal)


def halves(table):
    high = table.astype(np.float32).astype(ml_dtypes.bfloat16)
    low = (table - high.astype(np.float64)).astype(np.float32).astype(ml_dtypes.bfloat16)
    return high, low


def cas_np(length):
    phases = np.outer(np.arange(length), np.arange(length)) % length
    angles = phases * (2.0 * np.pi / length)
    return np.cos(angles) + np.sin(angles)


@functools.lru_cache(maxsize=None)
def tables(length, span_y, span_z, groups_y, groups_z):
    hart_x = cas_np(length)
    chunks = groups_y // 2
    hx = [
        np.ascontiguousarray(t.reshape(length, chunks, length // chunks).transpose(1, 0, 2))
        for t in halves(hart_x)
    ]
    hart_y = cas_np(span_y)
    forward = halves(hart_y * (-1.0 / (span_y * length)))
    backward = halves(hart_y)
    ty = np.stack([np.concatenate([hi, hi, lo], 1) for hi, lo in (forward, backward)])
    line_x = 4.0 * np.sin(np.pi * np.arange(length) / length) ** 2
    line_y = 4.0 * np.sin(np.pi * np.arange(span_y) / span_y) ** 2
    modes = (line_x[None, :] + line_y[:, None]).astype(np.float32)
    modes = np.ascontiguousarray(modes.reshape(span_y, groups_y, -1).transpose(1, 0, 2))
    k = np.arange(span_z)
    basis = np.cos(np.pi * np.outer(k, 2 * k + 1) / (2 * span_z))
    eig = 4.0 * np.sin(np.pi * k / (2 * span_z)) ** 2
    scale = np.where(k == 0, 0.0, 2.0 / (span_z * np.where(k == 0, 1.0, eig)))
    mean_free = (basis.T * scale) @ basis
    mean_free = mean_free.astype(np.float32).reshape(groups_z, -1, span_z)
    return hx[0], hx[1], ty, modes, mean_free


def split_rows(value):
    high = value.astype(jnp.bfloat16)
    return high, (value - high.astype(jnp.float32)).astype(jnp.bfloat16)


def dot32(a, b):
    return jnp.dot(a, b, preferred_element_type=jnp.float32)


def fused_kernel(
    ny, nz, motion, thermal, flow, base, hx_hi, hx_lo, ty_in, modes_in, free_in,
    out_p, out_t, out_pr, out_z,
    F, U, TH, HH, HL, TY, LAM, FREE, ZS, ZR, P0, P1, P2, PZS, PZR, S, A, B, D, PHI,
    R, MSG, MR, A2, B2, PR, QZS, QZR, OT, ZT, UZ, lsem, osem, ps, pr_, qs, qr, hs, hr, as_, ar, bs, br, zs, zr,
):
    gy, gz = lax.axis_index("gy"), lax.axis_index("gz")
    rows, layers, length = thermal.shape
    mesh_id = pl.DeviceIdType.MESH
    up_y, down_y = (gy + 1) % ny, (gy + ny - 1) % ny
    has_up, has_down = gz < nz - 1, gz > 0

    loads = [
        pltpu.make_async_copy(motion, F.at[0:3, 1 : rows + 1], lsem.at[0]),
        pltpu.make_async_copy(thermal, F.at[3, 1 : rows + 1], lsem.at[1]),
        pltpu.make_async_copy(base, TH, lsem.at[2]),
        pltpu.make_async_copy(flow, U, lsem.at[3]),
        pltpu.make_async_copy(modes_in.at[gy], LAM, lsem.at[4]),
        pltpu.make_async_copy(free_in.at[gz], FREE, lsem.at[5]),
        pltpu.make_async_copy(ty_in, TY, lsem.at[6]),
        pltpu.make_async_copy(hx_hi, HH, lsem.at[7]),
        pltpu.make_async_copy(hx_lo, HL, lsem.at[8]),
    ]
    for copy in loads:
        copy.start()

    barrier = pltpu.get_barrier_semaphore()
    for i in range(1, ny):
        pl.semaphore_signal(
            barrier, inc=1, device_id=((gy + i) % ny, gz), device_id_type=mesh_id
        )
    for i in range(1, nz):
        pl.semaphore_signal(
            barrier, inc=1, device_id=(gy, (gz + i) % nz), device_id_type=mesh_id
        )

    def remote(src, dst, ssem, rsem, y, z):
        return pltpu.make_async_remote_copy(
            src_ref=src, dst_ref=dst, send_sem=ssem, recv_sem=rsem,
            device_id=(y, z), device_id_type=mesh_id,
        )

    loads[2].wait()
    for y in range(rows):
        F[4, y + 1] = TH[y].astype(jnp.float32)
    loads[0].wait()
    loads[1].wait()
    for f in range(5):
        for y in range(rows):
            ZS[0, f, y : y + 1, :] = F[f, y + 1, 0:1, :]
            ZS[1, f, y : y + 1, :] = F[f, y + 1, layers - 1 : layers, :]
    pl.semaphore_wait(barrier, ny + nz - 2)

    z_down = remote(ZS.at[0], ZR.at[1], hs.at[0], hr.at[0], gy, gz - 1)
    z_up = remote(ZS.at[1], ZR.at[0], hs.at[1], hr.at[1], gy, gz + 1)
    y_down = remote(F.at[:, 1], F.at[:, rows + 1], hs.at[2], hr.at[2], down_y, gz)
    y_up = remote(F.at[:, rows], F.at[:, 0], hs.at[3], hr.at[3], up_y, gz)

    @pl.when(has_down)
    def _():
        z_down.start()

    @pl.when(has_up)
    def _():
        z_up.start()

    y_down.start()
    y_up.start()

    @pl.when(gz == 0)
    def _():
        ZR[0] = jnp.zeros_like(ZR[0])

    @pl.when(gz == nz - 1)
    def _():
        ZR[1] = jnp.zeros_like(ZR[1])
        PZR[...] = jnp.zeros_like(PZR)

    loads[4].wait()
    D[0] = jnp.zeros_like(D[0])

    def ratios(block, carry):
        def one(i, prod):
            at = block * layers + i
            e = LAM[...] + D[at]
            d = e / (1.0 + e)
            D[at + 1] = d
            return prod * (1.0 - d)

        PHI[block] = lax.fori_loop(0, layers, one, jnp.ones_like(LAM[...]))
        return carry

    lax.fori_loop(0, nz, ratios, 0)

    loads[3].wait()
    for y in range(rows):
        for i, f in enumerate((2, 4)):
            ZT[i, y : y + 1, :] = F[f, y + 1, 1:2, :]
        for d in range(3):
            UZ[d, y : y + 1, :] = U[d, y].astype(jnp.float32)[0:1, :]

    @pl.when(has_up)
    def _():
        z_down.wait_recv()

    @pl.when(has_down)
    def _():
        z_up.wait_recv()

    zi = lax.broadcasted_iota(jnp.int32, (layers, length), 0)

    def stencil(y, carry):
        def sides(f):
            c = F[f, y + 1]
            xp, xm = pltpu.roll(c, length - 1, 1), pltpu.roll(c, 1, 1)
            zp = jnp.where(zi == layers - 1, ZR[1, f, pl.ds(y, 1), :], pltpu.roll(c, layers - 1, 0))
            zm = jnp.where(zi == 0, ZR[0, f, pl.ds(y, 1), :], pltpu.roll(c, 1, 0))
            return c, xp, xm, F[f, y + 2], F[f, y], zp, zm

        u0, u1, u2 = (U[d, y].astype(jnp.float32) for d in range(3))

        def advance(f):
            c, xp, xm, yp, ym, zp, zm = sides(f)
            adv = 0.5 * (u0 * (xp - xm) + u1 * (yp - ym) + u2 * (zp - zm))
            lap = (xp + xm) + (yp + ym) + (zp + zm) - 6.0 * c
            return c, adv + viscosity * lap

        c3, t3 = advance(3)
        _, hxp, hxm, hyp, hym, hzp, hzm = sides(4)
        half = 0.5 * c3
        c, t = advance(0)
        P0[y] = c + time_step * (t + half * (hxp - hxm))
        c, t = advance(1)
        P1[y] = c + time_step * (t + half * (hyp - hym))
        c, t = advance(2)
        p2 = c + time_step * (t + half * (hzp - hzm))
        P2[y] = p2
        OT[y] = c3 + time_step * (t3 + buoyancy * c)
        return carry

    p1_down = remote(P1.at[0], P1.at[rows], hs.at[4], hr.at[4], down_y, gz)
    p2_down = remote(PZS, PZR, hs.at[5], hr.at[5], gy, gz - 1)
    inner = rows - 2
    lax.fori_loop(1, inner, stencil, 0)
    y_down.wait_recv()
    y_up.wait_recv()
    stencil(0, 0)
    p1_down.start()

    yi = lax.broadcasted_iota(jnp.int32, (rows, length), 0)
    c = ZS[0, 2]
    xp, xm = pltpu.roll(c, length - 1, 1), pltpu.roll(c, 1, 1)
    yp = jnp.where(yi == rows - 1, F[2, rows + 1, 0:1, :], pltpu.roll(c, rows - 1, 0))
    ym = jnp.where(yi == 0, F[2, 0, 0:1, :], pltpu.roll(c, 1, 0))
    zp, zm = ZT[0], ZR[0, 2]
    adv = 0.5 * (UZ[0] * (xp - xm) + UZ[1] * (yp - ym) + UZ[2] * (zp - zm))
    lap = (xp + xm) + (yp + ym) + (zp + zm) - 6.0 * c
    PZS[...] = c + time_step * (
        adv + viscosity * lap + 0.5 * ZS[0, 3] * (ZT[1] - ZR[0, 4])
    )

    @pl.when(has_down)
    def _():
        p2_down.start()

    lax.fori_loop(inner, rows, stencil, 0)
    outs = [
        pltpu.make_async_copy(OT, out_t, osem.at[0]),
        pltpu.make_async_copy(P0, out_p.at[0], osem.at[1]),
        pltpu.make_async_copy(P1.at[0:rows], out_p.at[1], osem.at[2]),
        pltpu.make_async_copy(P2, out_p.at[2], osem.at[3]),
    ]
    for copy in outs:
        copy.start()

    @pl.when(has_up)
    def _():
        p2_down.wait_recv()

    p1_down.wait_recv()
    half_rows = rows * layers

    def diverge(y, carry):
        p0, p2 = P0[y], P2[y]
        zp = jnp.where(zi == layers - 1, PZR[pl.ds(y, 1), :], pltpu.roll(p2, layers - 1, 0))
        s = (pltpu.roll(p0, length - 1, 1) - p0) + (P1[y + 1] - P1[y]) + (zp - p2)
        high, low = split_rows(s)
        S[pl.ds(pl.multiple_of(y * layers, layers), layers), :] = high
        S[pl.ds(pl.multiple_of(half_rows + y * layers, layers), layers), :] = low
        return carry

    lax.fori_loop(0, rows, diverge, 0)

    loads[7].wait()
    loads[8].wait()
    chunks = ny // 2

    def x_forward(i, carry):
        c = (gy // 2 + 1 + i) % chunks
        wide = dot32(S[...], HH[c])
        part = wide[:half_rows] + wide[half_rows:] + dot32(S[0:half_rows, :], HL[c])
        for side in range(2):
            peer = 2 * c + side
            A[peer] = part[:, side * 128 : (side + 1) * 128]

            @pl.when(peer != gy)
            def _():
                remote(A.at[peer], B.at[gy], as_.at[peer], ar.at[gy], peer, gz).start()

            @pl.when(peer == gy)
            def _():
                B[peer] = A[peer]

        return carry

    lax.fori_loop(0, chunks, x_forward, 0)
    loads[5].wait()
    loads[6].wait()

    def wait_all(src, dst, ssem, rsem):
        def one(i, carry):
            peer = (gy + i) % ny
            remote(src.at[peer], dst.at[peer], ssem.at[peer], rsem.at[peer], peer, gz).wait_recv()
            return carry

        lax.fori_loop(1, ny, one, 0)

    wait_all(A, B, as_, ar)
    span_y = ny * rows
    flat = B.reshape(ny * half_rows, 128)

    def y_transform(pair, table):
        high, low = split_rows(pair)
        return dot32(table, jnp.concatenate([high, low, high], 0))

    f_sweep = None
    start = gz * layers
    total = nz * layers
    for z in range(0, layers, 2):
        pair = jnp.concatenate(
            [flat[pl.ds(z + k, span_y, stride=layers), :] for k in range(2)], 1
        )
        res = y_transform(pair, TY[0])
        for k in range(2):
            r = res[:, k * 128 : (k + 1) * 128]
            R[z + k] = r
            MSG[0, span_y + z + k : span_y + z + k + 1, :] = r[0:1, :]
            MSG[1, span_y + z + k : span_y + z + k + 1, :] = r[0:1, :]
            w = 1.0 - D[start + z + k + 1]
            f_sweep = w * (r if f_sweep is None else r + f_sweep)
    MSG[0, 0:span_y, :] = f_sweep
    g_sweep = jnp.zeros_like(f_sweep)
    for z in range(layers - 1, -1, -1):
        g_sweep = (1.0 - D[total - start - z]) * (R[z] + g_sweep)
    MSG[1, 0:span_y, :] = g_sweep

    for i in range(1, nz):
        peer = (gz + i) % nz

        @pl.when(peer > gz)
        def _():
            remote(MSG.at[0], MR.at[gz], zs.at[peer], zr.at[gz], gy, peer).start()

        @pl.when(peer < gz)
        def _():
            remote(MSG.at[1], MR.at[gz], zs.at[peer], zr.at[gz], gy, peer).start()

    MR[gz] = MSG[0]
    for i in range(1, nz):
        peer = (gz + i) % nz
        remote(MSG.at[0], MR.at[peer], zs.at[peer], zr.at[peer], gy, peer).wait_recv()

    f = jnp.zeros_like(f_sweep)
    g = jnp.zeros_like(f_sweep)
    for s in range(nz):
        f = jnp.where(s < gz, MR[s, 0:span_y, :] + PHI[s] * f, f)
    for s in range(nz - 1, -1, -1):
        g = jnp.where(s > gz, MR[s, 0:span_y, :] + PHI[nz - 1 - s] * g, g)
    line = jnp.concatenate([MR[s, span_y:, :] for s in range(nz)], 0)
    level = jnp.dot(FREE[...], line, precision=highest, preferred_element_type=jnp.float32)
    plain = LAM[...] > 0.0
    for z in range(layers):
        f = (1.0 - D[start + z + 1]) * (R[z] + f)
        R[z] = f
    d_low, d_high = D[start + layers], D[total - start - layers]
    below = d_low + d_high - d_low * d_high
    p = (f + (1.0 - d_low) * g) / jnp.where(plain, below, 1.0)
    R[layers - 1] = p
    for z in range(layers - 2, -1, -1):
        p = (1.0 - D[start + z + 1]) * p + R[z]
        R[z] = p
    flat2 = A2.reshape(ny * half_rows, 128)
    for z in range(0, layers, 2):
        pair = jnp.concatenate(
            [jnp.where(plain, R[z + k], level[z + k : z + k + 1, :]) for k in range(2)], 1
        )
        res = y_transform(pair, TY[1])
        for k in range(2):
            flat2[pl.ds(z + k, span_y, stride=layers), :] = res[:, k * 128 : (k + 1) * 128]

    def send_back(i, carry):
        peer = (gy + i) % ny
        remote(A2.at[peer], B2.at[gy], bs.at[peer], br.at[gy], peer, gz).start()
        return carry

    lax.fori_loop(1, ny, send_back, 0)
    B2[gy] = A2[gy]

    width = length // chunks

    def edge(c):
        cols = slice(c * width, (c + 1) * width)
        return (
            remote(
                PR.at[rows, :, cols], PR.at[0, :, cols], ps.at[c], pr_.at[c], up_y, gz
            ),
            remote(QZS.at[:, cols], QZR.at[:, cols], qs.at[c], qr.at[c], gy, gz + 1),
        )

    for i in range(chunks):
        k = (gy // 2 + chunks - i) % chunks
        for side in range(2):
            peer = 2 * k + side

            @pl.when(peer != gy)
            def _():
                remote(
                    A2.at[peer], B2.at[peer], bs.at[peer], br.at[peer], peer, gz
                ).wait_recv()

        high, low = split_rows(jnp.concatenate([B2[2 * k], B2[2 * k + 1]], 1))
        both = jnp.concatenate([high, low], 0)
        span = pl.ds(pl.multiple_of(k * 256, 256), 256)
        for c in range(chunks):
            wide = dot32(both, HH[c, span, :])
            part = wide[:half_rows] + wide[half_rows:] + dot32(high, HL[c, span, :])
            part = part.reshape(rows, layers, width)
            cols = slice(c * width, (c + 1) * width)
            if i:
                part = part + PR[1 : rows + 1, :, cols]
            PR[1 : rows + 1, :, cols] = part
            if i == chunks - 1:
                QZS[:, cols] = jnp.concatenate(
                    [part[y, layers - 1 : layers, :] for y in range(rows)], 0
                )
                pr_up, pz_up = edge(c)
                pr_up.start()

                @pl.when(has_up)
                def _():
                    pz_up.start()

    @pl.when(gz == 0)
    def _():
        for y in range(rows):
            QZR[y : y + 1, :] = PR[y + 1, 0:1, :]

    for c in range(chunks):
        pr_up, pz_up = edge(c)
        pr_up.wait_recv()

        @pl.when(has_down)
        def _():
            pz_up.wait_recv()

    last = [
        pltpu.make_async_copy(PR, out_pr, osem.at[4]),
        pltpu.make_async_copy(QZR, out_z, osem.at[5]),
    ]
    for copy in last:
        copy.start()

    @pl.when(has_down)
    def _():
        z_down.wait_send()
        p2_down.wait_send()

    @pl.when(has_up)
    def _():
        z_up.wait_send()
        for c in range(chunks):
            edge(c)[1].wait_send()

    for c in range(chunks):
        edge(c)[0].wait_send()
    for copy in (y_down, y_up, p1_down):
        copy.wait_send()

    def finish(i, carry):
        peer = (gy + i) % ny
        remote(A.at[peer], B.at[gy], as_.at[peer], ar.at[gy], peer, gz).wait_send()
        remote(A2.at[peer], B2.at[gy], bs.at[peer], br.at[gy], peer, gz).wait_send()
        return carry

    lax.fori_loop(1, ny, finish, 0)
    for i in range(1, nz):
        peer = (gz + i) % nz
        remote(MSG.at[0], MR.at[gz], zs.at[peer], zr.at[gz], gy, peer).wait_send()
    for copy in outs + last:
        copy.wait()


def project_kernel(prov, pressure, lower, thermal, out_motion, out_thermal):
    _, count, layers, length = prov.shape
    first = pl.program_id(0) * count
    zi = lax.broadcasted_iota(jnp.int32, (layers, length), 0)
    for y in range(count):
        p = pressure[first + y + 1]
        zm = jnp.where(zi == 0, lower[pl.ds(first + y, 1), :], pltpu.roll(p, 1, 0))
        out_motion[0, y] = prov[0, y] - (p - pltpu.roll(p, 1, 1))
        out_motion[1, y] = prov[1, y] - (p - pressure[first + y])
        out_motion[2, y] = prov[2, y] - (p - zm)
    out_thermal[...] = thermal[...]


def fused_step(ny, nz, motion, thermal, flow, base):
    rows, layers, length = thermal.shape
    span_y, span_z = ny * rows, nz * layers
    constants = [jnp.asarray(t) for t in tables(length, span_y, span_z, ny, nz)]
    f32, b16 = jnp.float32, jnp.bfloat16
    flat = rows * layers
    vmem, dma = pltpu.VMEM, pltpu.SemaphoreType.DMA
    scratch = [
        vmem((5, rows + 2, layers, length), f32),
        vmem(flow.shape, b16),
        vmem(base.shape, b16),
        vmem(constants[0].shape, b16),
        vmem(constants[1].shape, b16),
        vmem(constants[2].shape, b16),
        vmem((span_y, 128), f32),
        vmem((layers, span_z), f32),
        vmem((2, 5, rows, length), f32),
        vmem((2, 5, rows, length), f32),
        vmem((rows, layers, length), f32),
        vmem((rows + 1, layers, length), f32),
        vmem((rows, layers, length), f32),
        vmem((rows, length), f32),
        vmem((rows, length), f32),
        vmem((2 * flat, length), b16),
        vmem((ny, flat, 128), f32),
        vmem((ny, flat, 128), f32),
        vmem((span_z + 1, span_y, 128), f32),
        vmem((nz, span_y, 128), f32),
        vmem((layers, span_y, 128), f32),
        vmem((2, span_y + layers, 128), f32),
        vmem((nz, span_y + layers, 128), f32),
        vmem((ny, flat, 128), f32),
        vmem((ny, flat, 128), f32),
        vmem((rows + 1, layers, length), f32),
        vmem((rows, length), f32),
        vmem((rows, length), f32),
        vmem((rows, layers, length), f32),
        vmem((2, rows, length), f32),
        vmem((3, rows, length), f32),
        dma((9,)),
        dma((6,)),
        dma((ny // 2,)),
        dma((ny // 2,)),
        dma((ny // 2,)),
        dma((ny // 2,)),
        dma((6,)),
        dma((6,)),
        dma((ny,)),
        dma((ny,)),
        dma((ny,)),
        dma((ny,)),
        dma((nz,)),
        dma((nz,)),
    ]
    hbm = pl.BlockSpec(memory_space=pltpu.HBM)
    prov, advanced, pressure, lower = pl.pallas_call(
        functools.partial(fused_kernel, ny, nz),
        out_shape=(
            jax.ShapeDtypeStruct(motion.shape, f32),
            jax.ShapeDtypeStruct(thermal.shape, f32),
            jax.ShapeDtypeStruct((rows + 1, layers, length), f32),
            jax.ShapeDtypeStruct((rows, length), f32),
        ),
        in_specs=[hbm] * 9,
        out_specs=(hbm,) * 4,
        scratch_shapes=scratch,
        compiler_params=pltpu.CompilerParams(
            collective_id=0, has_side_effects=True, vmem_limit_bytes=62 * 2**20
        ),
        cost_estimate=pl.CostEstimate(
            flops=12 * flat * length * length, bytes_accessed=10 * 2**20, transcendentals=0
        ),
    )(motion, thermal, flow, base, *constants)
    count = rows // 2
    fields = pl.BlockSpec((3, count, layers, length), lambda i: (0, i, 0, 0))
    single = pl.BlockSpec((count, layers, length), lambda i: (i, 0, 0))
    return pl.pallas_call(
        project_kernel,
        grid=(2,),
        out_shape=(
            jax.ShapeDtypeStruct(motion.shape, f32),
            jax.ShapeDtypeStruct(thermal.shape, f32),
        ),
        in_specs=[
            fields,
            pl.BlockSpec((rows + 1, layers, length), lambda i: (0, 0, 0)),
            pl.BlockSpec((rows, length), lambda i: (0, 0)),
            single,
        ],
        out_specs=(fields, single),
        compiler_params=pltpu.CompilerParams(vmem_limit_bytes=62 * 2**20),
    )(prov, pressure, lower, advanced)


def solution(mesh):
    placed = (
        P(None, "gy", "gz", None),
        P("gy", "gz", None),
        P(None, "gy", "gz", None),
        P("gy", "gz", None),
    )
    groups_y, groups_z = mesh.shape["gy"], mesh.shape["gz"]

    def step(motion, thermal, flow, base):
        rows, layers, length = thermal.shape
        if length == 128 * groups_y and groups_y % 2 == 0 and rows == 8 and layers == 16:
            return fused_step(groups_y, groups_z, motion, thermal, flow, base)
        return on_device(motion, thermal, flow, base)

    return jax.shard_map(
        step,
        mesh=mesh,
        in_specs=placed,
        out_specs=(P(None, "gy", "gz", None), P("gy", "gz", None)),
        check_vma=False,
    )
```
